128 devices in a mesh: case: 4 (over z_hi, core), gx: 8 (over y, z_lo), gy: 4 (over x).
Axes of the slice: x: 4, y: 4, z: 4 (z_hi: 2, z_lo: 2; z = z_hi * 2 + z_lo), core: 2. Of those that a mesh axis runs over, the one named last changes fastest.
Arguments:
- velocity: bfloat16 [4, 3, 128, 64, 128], P('case', None, 'gx', 'gy'), may hold values from -4 to 3
- target: bfloat16 [4, 3, 128, 64, 128], P('case', None, 'gx', 'gy'), may hold values from -3 to 3
- weight_in: bfloat16 [256, 12], replicated, may hold values from -1.75 to 1.75
- bias_in: float32 [256], replicated, may hold values from -3 to 3
- weight_mid: bfloat16 [256, 256], replicated, may hold values from -0.375 to 0.375
- bias_mid: float32 [256], replicated, may hold values from -3 to 3
- weight_out: bfloat16 [3, 256], replicated, may hold values from -0.375 to 0.375
- bias_out: float32 [3], replicated, may hold values from -3 to 3
- thrust_coef: float32 [100], replicated, may hold values from 0.5 to 1
- tile_cells: int32 [256, 128], P(('gx', 'gy')), may hold values from 0 to 32767
- tile_turbine: int32 [256], P(('gx', 'gy')), may hold values from -1 to 99, as said below
- tile_weight: float32 [256, 128], P(('gx', 'gy')), may hold values from 0.25 to 2
Outputs:
- velocity_new: bfloat16 [4, 3, 128, 64, 128], P('case', None, 'gx', 'gy')
- loss: float32 [], replicated
- step_weight_in: float32 [256, 12], replicated
- step_bias_in: float32 [256], replicated
- step_weight_mid: float32 [256, 256], replicated
- step_bias_mid: float32 [256], replicated
- step_weight_out: float32 [3, 256], replicated
- step_bias_out: float32 [3], replicated
- force_grad: bfloat16 [4, 3, 128, 64, 128], P('case', None, 'gx', 'gy')
The draws below stay inside these ranges and needn't reach their ends.
Inputs may be any that keep to these rules, and one draw needn't show every extreme that they name: `tile_turbine`: in each device's block of 8 tile rows the used rows come first and the rest hold -1; in every draw some device has all 8 rows used.
All inputs are finite; a program needn't handle non-finite values.
Results may differ from the reference program's by a relative error of at most 0.0006.
The reference program's roundings to bfloat16 on the way (of `features`, `hidden_one`, `hidden_two`, `provisional`, `delta_two` and `delta_one`) count: a program that leaves them out, or rounds other values in their place, can miss the bound.
Values may be sent and summed in bfloat16 or wider, within the bound.
A program may use at most 128 MiB of HBM per device.

```python
import math
import jax
import jax.numpy as jnp
from jax import lax

CX = 16
CY = 16
NZ = 128
UNITS = 256
FEATS = 12
TURBINES = 100
TILES_DEV = 8
DISK_ROW = 128
ITERS = 20
CASES = 4
NX = 128
NY = 64
TILES = 256
N_GX = 8
N_GY = 4


def draw_tile_turbine(key, part):
    block_total = TILES // TILES_DEV
    count_key, full_key, turbine_key = jax.random.split(jax.random.fold_in(key, 17), 3)
    row_counts = jax.random.randint(count_key, (block_total,), 0, TILES_DEV + 1)
    full_block = jax.random.randint(full_key, (), 0, block_total)
    row_counts = jnp.where(jnp.arange(block_total) == full_block, TILES_DEV, row_counts)
    turbine_ids = jax.random.randint(turbine_key, (block_total, TILES_DEV), 0, TURBINES)
    live_rows = jnp.arange(TILES_DEV)[None, :] < row_counts[:, None]
    return jnp.where(live_rows, turbine_ids, -1).reshape(TILES).astype(jnp.int32)


def draw_velocity(key, part):
    noise_key = jax.random.fold_in(key, 29)
    shape = (CASES, 3, NX, NY, NZ)
    place = jnp.arange(NX, dtype=jnp.float32) / float(max(NX - 1, 1))
    noise = jnp.clip(0.5 * jax.random.normal(noise_key, shape, jnp.float32), -2.4, 2.4)
    deficit = -0.8 * place
    stream = (jnp.arange(3) == 0).astype(jnp.float32)[:, None, None, None]
    values = noise + stream * deficit[None, :, None, None]
    return values.astype(jnp.bfloat16)


def plant(values, stream_key, low, high):
    longest = values.shape.index(max(values.shape))
    spots = []
    for shift in (0, 1):
        where = [jax.random.randint(jax.random.fold_in(stream_key, axis), (), 0, length) for axis, length in enumerate(values.shape)]
        where[longest] = (where[longest] + shift) % values.shape[longest]
        spots.append(tuple(where))
    return values.at[spots[0]].set(low).at[spots[1]].set(high)


def steps_of(key, dims, pieces, low, top_value):
    loudness = 1.0
    for dim, blocks in pieces:
        draws = jax.random.uniform(jax.random.fold_in(jax.random.fold_in(key, 6), dim), (blocks,), jnp.float32, low / len(pieces), top_value / len(pieces))
        loudness = loudness * jnp.repeat(jnp.exp(draws), dims[dim] // blocks).reshape((-1,) + (1,) * (len(dims) - 1 - dim))
    return loudness


def gaussian(key, dims, scale, bound, pieces=(), kind=jnp.bfloat16):
    result = jax.random.normal(key, dims, jnp.float32) * scale
    if len(pieces) > 0:
        result = steps_of(key, dims, pieces, -0.22, 0.18) * result
    return jnp.clip(result, min=-bound, max=bound).astype(kind)


def setup_inputs(seed: int = 0) -> dict:
    arg_keys = jax.random.split(jax.random.key(seed), 13)
    velocity = draw_velocity(jax.random.fold_in(arg_keys[12], 71), 0)
    target = gaussian(arg_keys[1], (CASES, 3, NX, NY, NZ), 0.5, 3.0, ((0, 4), (2, 8), (3, 4)))
    weight_in = gaussian(arg_keys[2], (UNITS, FEATS), FEATS ** -0.5, 1.75)
    bias_in = gaussian(arg_keys[3], (UNITS,), 0.5, 3.0, (), jnp.float32)
    weight_mid = gaussian(arg_keys[4], (UNITS, UNITS), UNITS ** -0.5, 0.375)
    bias_mid = gaussian(arg_keys[5], (UNITS,), 0.5, 3.0, (), jnp.float32)
    weight_out = gaussian(arg_keys[6], (3, UNITS), UNITS ** -0.5, 0.375)
    bias_out = gaussian(arg_keys[7], (3,), 0.5, 3.0, (), jnp.float32)
    thrust_coef = jnp.clip(jax.random.uniform(arg_keys[8], (TURBINES,), jnp.float32, 0.5, 1.0), 0.5, 1.0)
    tile_cells = plant(jax.random.randint(arg_keys[9], (TILES, DISK_ROW), 0, CX * CY * NZ), jax.random.fold_in(arg_keys[9], 1), 0, (CX * CY * NZ) - 1).astype(jnp.int32)
    tile_turbine = draw_tile_turbine(jax.random.fold_in(arg_keys[12], 71), 0)
    tile_weight = jnp.clip(jnp.exp(math.log(2.0) - 2.0794415 * jax.random.uniform(arg_keys[11], (TILES, DISK_ROW), jnp.float32) ** steps_of(arg_keys[11], (TILES, DISK_ROW), ((0, 32),), -0.2, 0.2)), 0.25, 2.0)
    return {"velocity": velocity, "target": target, "weight_in": weight_in, "bias_in": bias_in, "weight_mid": weight_mid, "bias_mid": bias_mid, "weight_out": weight_out, "bias_out": bias_out, "thrust_coef": thrust_coef, "tile_cells": tile_cells, "tile_turbine": tile_turbine, "tile_weight": tile_weight}


inflow = 1.0
step_dt = 0.4
viscosity = 0.1
epsilon_rms = 1e-06

def offset_view(extended, spatial_dim, offset):
    slicers = [slice(None)] * (extended.ndim - 3)
    for position in range(3):
        length = extended.shape[extended.ndim - 3 + position]
        if position == spatial_dim:
            slicers.append(slice(1 + offset, length - 1 + offset))
        else:
            slicers.append(slice(1, length - 1))
    return extended[tuple(slicers)]

def central(extended, spatial_dim):
    return 0.5 * (offset_view(extended, spatial_dim, 1) - offset_view(extended, spatial_dim, -1))

def neighbour_sum(extended):
    summed = offset_view(extended, 0, 1) + offset_view(extended, 0, -1)
    for spatial_dim in (1, 2):
        summed = summed + offset_view(extended, spatial_dim, 1) + offset_view(extended, spatial_dim, -1)
    return summed

def pad_all(values):
    padding = [(0, 0)] * (values.ndim - 3) + [(1, 1)] * 3
    return jnp.pad(values, padding)

def contract_cells(former, latter):
    return lax.dot_general(former, latter, (((1,), (1,)), ((), ())), preferred_element_type=jnp.float32)

def to_blocks(values):
    leading = values.shape[:-3]
    lead_count = len(leading)
    shaped = values.reshape(leading + (N_GX, CX, N_GY, CY, NZ))
    order = (lead_count, lead_count + 2) + tuple(range(lead_count)) + (lead_count + 1, lead_count + 3, lead_count + 4)
    return jnp.transpose(shaped, order).reshape((N_GX * N_GY,) + leading + (CX * CY * NZ,))

def from_blocks(blocked):
    leading = blocked.shape[1:-1]
    lead_count = len(leading)
    shaped = blocked.reshape((N_GX, N_GY) + leading + (CX, CY, NZ))
    order = tuple(range(2, 2 + lead_count)) + (0, lead_count + 2, 1, lead_count + 3, lead_count + 4)
    return jnp.transpose(shaped, order).reshape(leading + (NX, NY, NZ))

def divergence_of(extended):
    return central(extended[0], 0) + central(extended[1], 1) + central(extended[2], 2)

def pressure_correction(divergence):
    source = divergence / step_dt

    def sweep(sweep_number, pressure):
        return (neighbour_sum(pad_all(pressure)) - source) / 6.0
    pressure = lax.fori_loop(0, ITERS, sweep, jnp.zeros_like(source))
    padded = pad_all(pressure)
    return step_dt * jnp.stack([central(padded, spatial_dim) for spatial_dim in range(3)])

def closure_forward(features_block, weight_in, bias_in, weight_mid, bias_mid, weight_out, bias_out):
    hidden_one = jnp.tanh(jnp.dot(weight_in, features_block, preferred_element_type=jnp.float32) + bias_in[:, None]).astype(jnp.bfloat16)
    hidden_two = jnp.tanh(jnp.dot(weight_mid, hidden_one, preferred_element_type=jnp.float32) + bias_mid[:, None]).astype(jnp.bfloat16)
    closure = jnp.dot(weight_out, hidden_two, preferred_element_type=jnp.float32) + bias_out[:, None]
    return (hidden_one, hidden_two, closure)

def closure_backward(features_block, force_grad, hidden_one, hidden_two, weight_mid, weight_out):
    grad_weight_out = contract_cells(force_grad, hidden_two)
    grad_bias_out = lax.optimization_barrier(jnp.sum(force_grad.astype(jnp.float32), 1))
    back_two = jnp.dot(weight_out.T, force_grad, preferred_element_type=jnp.float32)
    two_value = hidden_two.astype(jnp.float32)
    delta_two = (back_two * (1.0 - two_value * two_value)).astype(jnp.bfloat16)
    grad_weight_mid = contract_cells(delta_two, hidden_one)
    grad_bias_mid = lax.optimization_barrier(jnp.sum(delta_two.astype(jnp.float32), 1))
    back_one = jnp.dot(weight_mid.T, delta_two, preferred_element_type=jnp.float32)
    one_value = hidden_one.astype(jnp.float32)
    delta_one = (back_one * (1.0 - one_value * one_value)).astype(jnp.bfloat16)
    grad_weight_in = contract_cells(delta_one, features_block)
    grad_bias_in = lax.optimization_barrier(jnp.sum(delta_one.astype(jnp.float32), 1))
    return (grad_weight_in, grad_bias_in, grad_weight_mid, grad_bias_mid, grad_weight_out, grad_bias_out)

def reference(velocity, target, weight_in, bias_in, weight_mid, bias_mid, weight_out, bias_out, thrust_coef, tile_cells, tile_turbine, tile_weight):
    cells_dev = CX * CY * NZ
    block_total = N_GX * N_GY
    params = (weight_in, bias_in, weight_mid, bias_mid, weight_out, bias_out)
    totals = (jnp.zeros((UNITS, FEATS), jnp.float32), jnp.zeros((UNITS,), jnp.float32), jnp.zeros((UNITS, UNITS), jnp.float32), jnp.zeros((UNITS,), jnp.float32), jnp.zeros((3, UNITS), jnp.float32), jnp.zeros((3,), jnp.float32))
    cost = jnp.zeros((), jnp.float32)
    new_fields = []
    force_fields = []
    matches = (tile_turbine[:, None] == jnp.arange(TURBINES, dtype=jnp.int32)[None, :]).astype(jnp.float32)
    cell_rows = tile_cells.reshape(block_total, TILES_DEV * DISK_ROW).astype(jnp.int32)
    weight_sums = lax.optimization_barrier(jnp.sum(tile_weight, 1))

    def forward_block(features_block):
        return closure_forward(features_block, *params)[2]

    def accumulate(carry, inputs):
        features_block, force_block = inputs
        hidden_one, hidden_two, unused = closure_forward(features_block, *params)
        grads = closure_backward(features_block, force_block, hidden_one, hidden_two, weight_mid, weight_out)
        return (jax.tree.map(lambda first_term, second_term: first_term + second_term, carry, grads), None)

    def scatter_block(rows_here, values_here):
        return jnp.zeros((cells_dev,), jnp.float32).at[rows_here].add(values_here)
    for case_index in range(CASES):
        velocity_case = velocity[case_index]
        extended = pad_all(velocity_case).astype(jnp.float32)
        gradients = [central(extended, spatial_dim) for spatial_dim in range(3)]
        fluctuation = velocity_case.astype(jnp.float32)
        full_speed = fluctuation.at[0].add(inflow)
        features = jnp.concatenate(gradients + [fluctuation], 0).astype(jnp.bfloat16)
        feature_blocks = to_blocks(features)
        closure = from_blocks(lax.map(forward_block, feature_blocks))
        stream_blocks = to_blocks(full_speed[0])
        sampled = jnp.take_along_axis(stream_blocks, cell_rows, axis=1).reshape(TILES, DISK_ROW)
        weighted = lax.optimization_barrier(jnp.sum(tile_weight * sampled, 1))
        disk_sum = lax.optimization_barrier(jnp.sum(matches * weighted[:, None], 0))
        disk_area = lax.optimization_barrier(jnp.sum(matches * weight_sums[:, None], 0))
        disk_speed = disk_sum / jnp.maximum(disk_area, 1.0)
        thrust = -0.5 * thrust_coef * disk_speed * jnp.abs(disk_speed)
        row_thrust = lax.optimization_barrier(jnp.sum(matches * thrust[None, :], 1))
        spread = (tile_weight * row_thrust[:, None]).reshape(block_total, TILES_DEV * DISK_ROW)
        turbine_force = from_blocks(jax.vmap(scatter_block)(cell_rows, spread))
        laplace = neighbour_sum(extended) - 6.0 * fluctuation
        advect = full_speed[0] * gradients[0] + full_speed[1] * gradients[1] + full_speed[2] * gradients[2]
        tendency = viscosity * laplace - advect + closure
        tendency = tendency.at[0].add(turbine_force)
        provisional = (fluctuation + step_dt * tendency).astype(jnp.bfloat16)
        rim = pad_all(provisional).astype(jnp.float32)
        updated = provisional.astype(jnp.float32) - pressure_correction(divergence_of(rim))
        new_fields.append(updated.astype(jnp.bfloat16))
        mismatch = updated - target[case_index].astype(jnp.float32)
        cost = cost + jnp.sum(mismatch * mismatch)
        seed_grad = 2.0 * mismatch
        adjoint = seed_grad - pressure_correction(divergence_of(pad_all(seed_grad)))
        force_field = (step_dt * adjoint).astype(jnp.bfloat16)
        force_fields.append(force_field)
        force_blocks = to_blocks(force_field)
        totals = lax.scan(accumulate, totals, (feature_blocks, force_blocks))[0]
    entry_total = UNITS * FEATS + UNITS + UNITS * UNITS + UNITS + 3 * UNITS + 3
    squares = sum((jnp.sum(grad_value * grad_value) for grad_value in totals))
    scale_rms = jnp.sqrt(squares / entry_total + epsilon_rms)
    loss = cost / (3 * CASES * NX * NY * NZ)
    velocity_new = jnp.stack(new_fields)
    force_grad = jnp.stack(force_fields)
    return (velocity_new, loss, totals[0] / scale_rms, totals[1] / scale_rms, totals[2] / scale_rms, totals[3] / scale_rms, totals[4] / scale_rms, totals[5] / scale_rms, force_grad)
```

```python
import functools
import math

import jax
import jax.numpy as jnp
import numpy as np
from jax import lax
from jax.experimental import pallas as pl
from jax.experimental.pallas import tpu as pltpu
from jax.sharding import PartitionSpec as P

ITERS = 20
MESH = pl.DeviceIdType.MESH
HIGHEST = lax.Precision.HIGHEST

inflow = 1.0
step_dt = 0.4
viscosity = 0.1
epsilon_rms = 1e-06

ROWS = 24
LIVE = 18
SLOTS = 32
FIRST = 8


def extended_2(block, sides, width):
    for axis, dim in sides:
        count = lax.axis_size(axis)
        forward = [(i, i + 1) for i in range(count - 1)]
        backward = [(target, source) for source, target in forward]
        low = lax.ppermute(
            lax.slice_in_dim(block, block.shape[dim] - width, None, axis=dim), axis, forward
        )
        high = lax.ppermute(lax.slice_in_dim(block, 0, width, axis=dim), axis, backward)
        block = jnp.concatenate([low, block, high], axis=dim)
    return block


def offset_view(extended, spatial_dim, offset):
    slicers = [slice(None)] * (extended.ndim - 3)
    for position in range(3):
        length = extended.shape[extended.ndim - 3 + position]
        if position == spatial_dim:
            slicers.append(slice(1 + offset, length - 1 + offset))
        else:
            slicers.append(slice(1, length - 1))
    return extended[tuple(slicers)]


def central(extended, spatial_dim):
    return 0.5 * (offset_view(extended, spatial_dim, 1) - offset_view(extended, spatial_dim, -1))


def neighbour_sum(extended):
    summed = offset_view(extended, 0, 1) + offset_view(extended, 0, -1)
    for spatial_dim in (1, 2):
        summed = (
            summed + offset_view(extended, spatial_dim, 1) + offset_view(extended, spatial_dim, -1)
        )
    return summed


def pad_depth(values, margin):
    padding = [(0, 0)] * (values.ndim - 1) + [(margin, margin)]
    return jnp.pad(values, padding)


def contract_cells(former, latter):
    return lax.dot_general(
        former, latter, (((1,), (1,)), ((), ())), preferred_element_type=jnp.float32
    )


def sines(count):
    index = np.arange(1, count + 1, dtype=np.float64)
    return math.sqrt(2.0 / (count + 1)) * np.sin(math.pi * np.outer(index, index) / (count + 1))


def cosines(count):
    return 2.0 * np.cos(math.pi * np.arange(1, count + 1, dtype=np.float64) / (count + 1))


def solve_tables(n_gx, n_gy, span_x, span_y, depth):
    nx, ny = n_gx * span_x, n_gy * span_y
    group = n_gx * n_gy
    modes = depth // group
    base_x, base_y = sines(nx), sines(ny)
    in_y = np.zeros((n_gy, modes, SLOTS, modes, ny))
    for gy in range(n_gy):
        for slot in range(FIRST - 1, FIRST + span_y + 1):
            y = gy * span_y + slot - FIRST
            if 0 <= y < ny:
                for mode in range(modes):
                    in_y[gy, mode, slot, mode] = base_y[y]
    in_y = in_y.reshape(n_gy * modes * SLOTS, modes * ny)
    in_x = np.zeros((nx, n_gx, ROWS))
    for gx in range(n_gx):
        for row in range(LIVE):
            x = gx * span_x + (row if row < span_x else (-1 if row == span_x else span_x))
            if 0 <= x < nx:
                in_x[:, gx, row] = base_x[x]
    in_x = in_x.reshape(nx, n_gx * ROWS)
    plane = np.tile((cosines(nx)[:, None] + cosines(ny)[None, :]) / 6.0, (1, modes))
    level = np.repeat((cosines(depth) / 6.0).reshape(modes, group).T, ny, axis=1)
    tables = (sines(depth), in_y, in_y.T, in_x, in_x.T, plane, level[:, None, :])
    return tuple(np.ascontiguousarray(table, dtype=np.float32) for table in tables)


def dot_full(left, right):
    return jnp.dot(left, right, precision=HIGHEST, preferred_element_type=jnp.float32)


def depth_difference(values):
    dim = values.ndim - 1
    depth = values.shape[dim]
    lane = lax.broadcasted_iota(jnp.int32, values.shape, dim)
    above = jnp.where(lane == depth - 1, 0.0, pltpu.roll(values, depth - 1, dim))
    below = jnp.where(lane == 0, 0.0, pltpu.roll(values, 1, dim))
    return above - below


def swap_groups(pieces, stride):
    count = len(pieces)
    lane = lax.broadcasted_iota(jnp.int32, pieces[0].shape, 1) // stride
    results = []
    for b in range(count):
        result = None
        for a in range(count):
            shift = ((a - b) * stride) % (count * stride)
            moved = pieces[a] if shift == 0 else pltpu.roll(pieces[a], shift, 1)
            result = moved if result is None else jnp.where(lane == a, moved, result)
        results.append(result)
    return results


def project_kernel(
    n_gx,
    n_gy,
    u_ref,
    t_ref,
    base_z,
    in_y,
    out_y,
    in_x,
    out_x,
    plane,
    level,
    new_ref,
    force_ref,
    cost_ref,
    rext,
    pext,
    field,
    gain,
    send_a,
    recv_a,
    send_b,
    recv_b,
    send_sem,
    recv_sem,
):
    case, gx, gy = lax.axis_index("case"), lax.axis_index("gx"), lax.axis_index("gy")
    group = n_gx * n_gy
    me = gy * n_gx + gx
    span_x, span_y, depth = u_ref.shape[1:]
    modes = depth // group

    def device(index):
        return (case, lax.rem(index, n_gx), index // n_gx)

    for side in range(2):
        recv_a[side, :, span_x:, :] = jnp.zeros((group, ROWS - span_x, depth), jnp.float32)

    barrier = pltpu.get_barrier_semaphore()

    def greet(step, carry):
        pl.semaphore_signal(
            barrier,
            inc=1,
            device_id=device(lax.rem(me + step, group)),
            device_id_type=MESH,
        )
        return carry

    lax.fori_loop(1, group, greet, 0)

    ratio = plane[...] + level[me]
    total = jnp.ones_like(ratio)
    for _ in range(ITERS - 1):
        total = total * ratio + 1.0
    gain[...] = total * (-1.0 / 24.0)
    rext[...] = jnp.zeros_like(rext)

    def exchange(number, outgoing, incoming):
        def start(step, carry):
            peer = lax.rem(me + step, group)
            pltpu.make_async_remote_copy(
                src_ref=outgoing.at[peer, pl.ds(0, LIVE)],
                dst_ref=incoming.at[me, pl.ds(0, LIVE)],
                send_sem=send_sem.at[number],
                recv_sem=recv_sem.at[number],
                device_id=device(peer),
                device_id_type=MESH,
            ).start()
            return carry

        lax.fori_loop(1, group, start, 0)
        incoming[me, pl.ds(0, LIVE)] = outgoing[me, pl.ds(0, LIVE)]
        landed = incoming.at[pl.ds(0, group - 1), pl.ds(0, LIVE)]
        pltpu.make_async_copy(landed, landed, recv_sem.at[number]).wait()

    def sent(number, outgoing):
        left = outgoing.at[pl.ds(0, group - 1), pl.ds(0, LIVE)]
        pltpu.make_async_copy(left, left, send_sem.at[number]).wait()

    def solve(number, q_x, q_y, q_z):
        zero_x = jnp.zeros((1, span_y, depth), jnp.float32)
        inner = jnp.concatenate([q_x[1:], zero_x], 0) - jnp.concatenate([zero_x, q_x[:-1]], 0)
        inner = inner + depth_difference(q_z)
        last = FIRST + span_y
        wide = jnp.concatenate(
            [
                jnp.zeros((span_x, FIRST, depth), jnp.float32),
                q_y,
                jnp.zeros((span_x, SLOTS - last, depth), jnp.float32),
            ],
            1,
        )
        rext[0:span_x] = pltpu.roll(wide, SLOTS - 1, 1) - pltpu.roll(wide, 1, 1)
        rext[0:span_x, FIRST:last, :] = rext[0:span_x, FIRST:last, :] + inner
        rext[span_x, FIRST:last, :] = q_x[0]
        rext[span_x + 1, FIRST:last, :] = -q_x[span_x - 1]
        if number > 0:
            sent(2 * number - 2, send_a)
        for part in range(rext.shape[0] // modes):
            cells = rext[part * modes : (part + 1) * modes].reshape(modes * SLOTS, depth)
            turned = dot_full(cells, base_z[...]).T
            pieces = [turned[m * group : (m + 1) * group] for m in range(modes)]
            for inside, piece in enumerate(swap_groups(pieces, SLOTS)):
                if part * modes + inside < LIVE:
                    send_a[:, part * modes + inside, :] = piece
        if number == 0:
            pl.semaphore_wait(barrier, group - 1)
        arrived = recv_a.at[number]
        exchange(2 * number, send_a, arrived)
        along_y = None
        for block in range(n_gy):
            rows = arrived[block * n_gx : (block + 1) * n_gx].reshape(n_gx * ROWS, depth)
            part = dot_full(rows, in_y[block * depth : (block + 1) * depth, :])
            along_y = part if along_y is None else along_y + part
        spectrum = dot_full(in_x[...], along_y) * gain[...]
        back = dot_full(out_x[...], spectrum)
        if number > 0:
            sent(2 * number - 1, send_b)
        for block in range(n_gy):
            part = dot_full(back, out_y[:, block * depth : (block + 1) * depth])
            send_b[block * n_gx : (block + 1) * n_gx] = part.reshape(n_gx, ROWS, depth)
        arrived = recv_b.at[number]
        exchange(2 * number + 1, send_b, arrived)
        for part in range(pext.shape[0] // modes):
            pieces = [
                arrived[:, min(part * modes + inside, LIVE - 1), :] for inside in range(modes)
            ]
            turned = jnp.concatenate(swap_groups(pieces, SLOTS), 0).T
            pext[part * modes : (part + 1) * modes] = dot_full(turned, base_z[...]).reshape(
                modes, SLOTS, depth
            )

    def slope():
        last = FIRST + span_y
        middle = pext[0:span_x, FIRST:last, :]
        low = pext[span_x : span_x + 1, FIRST:last, :]
        high = pext[span_x + 1 : span_x + 2, FIRST:last, :]
        along_x = jnp.concatenate([middle[1:], high], 0) - jnp.concatenate([low, middle[:-1]], 0)
        along_y = (
            pext[0:span_x, FIRST + 1 : last + 1, :] - pext[0:span_x, FIRST - 1 : last - 1, :]
        )
        return along_x, along_y, depth_difference(middle)

    solve(0, *[u_ref[component].astype(jnp.float32) for component in range(3)])
    cost = jnp.zeros((8, depth), jnp.float32)
    for component, change in enumerate(slope()):
        updated = u_ref[component].astype(jnp.float32) - change
        new_ref[component] = updated.astype(jnp.bfloat16)
        mismatch = updated - t_ref[component].astype(jnp.float32)
        cost = cost + jnp.sum((mismatch * mismatch).reshape(-1, 8, depth), 0)
        field[component] = 2.0 * mismatch
    cost_ref[...] = cost
    solve(1, field[0], field[1], field[2])
    for component, change in enumerate(slope()):
        force_ref[component] = (step_dt * (field[component] - change)).astype(jnp.bfloat16)
    sent(2, send_a)
    sent(3, send_b)


def project(provisional, target):
    n_gx, n_gy = lax.axis_size("gx"), lax.axis_size("gy")
    group = n_gx * n_gy
    _, span_x, span_y, depth = provisional.shape
    tables = solve_tables(n_gx, n_gy, span_x, span_y, depth)
    f32 = jnp.float32
    vmem = pl.BlockSpec(memory_space=pltpu.VMEM)
    return pl.pallas_call(
        functools.partial(project_kernel, n_gx, n_gy),
        out_shape=(
            jax.ShapeDtypeStruct(provisional.shape, jnp.bfloat16),
            jax.ShapeDtypeStruct(provisional.shape, jnp.bfloat16),
            jax.ShapeDtypeStruct((8, depth), f32),
        ),
        in_specs=[vmem] * (2 + len(tables)),
        out_specs=(vmem, vmem, vmem),
        scratch_shapes=[
            pltpu.VMEM((span_x + 4, SLOTS, depth), f32),
            pltpu.VMEM((span_x + 4, SLOTS, depth), f32),
            pltpu.VMEM((3, span_x, span_y, depth), f32),
            pltpu.VMEM(tables[5].shape, f32),
            pltpu.VMEM((group, ROWS, depth), f32),
            pltpu.VMEM((2, group, ROWS, depth), f32),
            pltpu.VMEM((group, ROWS, depth), f32),
            pltpu.VMEM((2, group, ROWS, depth), f32),
            pltpu.SemaphoreType.DMA((4,)),
            pltpu.SemaphoreType.DMA((4,)),
        ],
        compiler_params=pltpu.CompilerParams(
            collective_id=0, has_side_effects=True, vmem_limit_bytes=48 * 1024 * 1024
        ),
        name="project",
    )(provisional, target, *tables)


def reduce_kernel(sizes, part_ref, out_ref, recv, mine, send_sem, recv_sem):
    n_case, n_gx, n_gy = sizes
    total = n_case * n_gx * n_gy
    case, gx, gy = lax.axis_index("case"), lax.axis_index("gx"), lax.axis_index("gy")
    me = (case * n_gx + gx) * n_gy + gy

    def device(index):
        return (index // (n_gx * n_gy), lax.rem(index // n_gy, n_gx), lax.rem(index, n_gy))

    barrier = pltpu.get_barrier_semaphore()

    def greet(step, carry):
        pl.semaphore_signal(
            barrier, inc=1, device_id=device(lax.rem(me + step, total)), device_id_type=MESH
        )
        return carry

    lax.fori_loop(1, total, greet, 0)
    pl.semaphore_wait(barrier, total - 1)

    def scatter(step, carry):
        peer = lax.rem(me + step, total)
        pltpu.make_async_remote_copy(
            src_ref=part_ref.at[peer],
            dst_ref=recv.at[me],
            send_sem=send_sem.at[0],
            recv_sem=recv_sem.at[0],
            device_id=device(peer),
            device_id_type=MESH,
        ).start()
        return carry

    lax.fori_loop(1, total, scatter, 0)
    recv[me] = part_ref[me]
    others = recv.at[pl.ds(0, total - 1)]
    pltpu.make_async_copy(others, others, recv_sem.at[0]).wait()
    mine[...] = jnp.sum(recv[...], 0)

    def spread(step, carry):
        peer = lax.rem(me + step, total)
        pltpu.make_async_remote_copy(
            src_ref=mine,
            dst_ref=out_ref.at[me],
            send_sem=send_sem.at[1],
            recv_sem=recv_sem.at[1],
            device_id=device(peer),
            device_id_type=MESH,
        ).start()
        return carry

    lax.fori_loop(1, total, spread, 0)
    out_ref[me] = mine[...]
    others = out_ref.at[pl.ds(0, total - 1)]
    pltpu.make_async_copy(others, others, recv_sem.at[1]).wait()
    pltpu.make_async_copy(others, others, send_sem.at[0]).wait()
    pltpu.make_async_copy(others, others, send_sem.at[1]).wait()


def reduce_all(parts):
    sizes = (lax.axis_size("case"), lax.axis_size("gx"), lax.axis_size("gy"))
    vmem = pl.BlockSpec(memory_space=pltpu.VMEM)
    return pl.pallas_call(
        functools.partial(reduce_kernel, sizes),
        out_shape=jax.ShapeDtypeStruct(parts.shape, jnp.float32),
        in_specs=[vmem],
        out_specs=vmem,
        scratch_shapes=[
            pltpu.VMEM(parts.shape, jnp.float32),
            pltpu.VMEM(parts.shape[1:], jnp.float32),
            pltpu.SemaphoreType.DMA((2,)),
            pltpu.SemaphoreType.DMA((2,)),
        ],
        compiler_params=pltpu.CompilerParams(
            collective_id=1, has_side_effects=True, vmem_limit_bytes=16 * 1024 * 1024
        ),
        name="reduce_all",
    )(parts)


def on_device(
    velocity,
    target,
    weight_in,
    bias_in,
    weight_mid,
    bias_mid,
    weight_out,
    bias_out,
    thrust_coef,
    tile_cells,
    tile_turbine,
    tile_weight,
):
    velocity_case = velocity[0]
    span_x = velocity_case.shape[1]
    span_y = velocity_case.shape[2]
    depth = velocity_case.shape[3]
    cells_dev = span_x * span_y * depth
    turbine_total = thrust_coef.shape[0]
    extended = extended_2(velocity_case, (("gx", 1), ("gy", 2)), 1)
    extended = pad_depth(extended, 1).astype(jnp.float32)
    gradients = [central(extended, spatial_dim) for spatial_dim in range(3)]
    fluctuation = velocity_case.astype(jnp.float32)
    full_speed = fluctuation.at[0].add(inflow)
    features = (
        jnp.concatenate(gradients + [fluctuation], 0).reshape(12, cells_dev).astype(jnp.bfloat16)
    )
    hidden_one = jnp.tanh(
        jnp.dot(weight_in, features, preferred_element_type=jnp.float32) + bias_in[:, None]
    ).astype(jnp.bfloat16)
    hidden_two = jnp.tanh(
        jnp.dot(weight_mid, hidden_one, preferred_element_type=jnp.float32) + bias_mid[:, None]
    ).astype(jnp.bfloat16)
    closure = (
        jnp.dot(weight_out, hidden_two, preferred_element_type=jnp.float32) + bias_out[:, None]
    )
    stream_flat = full_speed[0].reshape(cells_dev)
    sampled = stream_flat[tile_cells]
    weighted = jnp.sum(tile_weight * sampled, 1)
    weight_sums = jnp.sum(tile_weight, 1)
    matches = (tile_turbine[:, None] == jnp.arange(turbine_total, dtype=jnp.int32)[None, :]).astype(
        jnp.float32
    )
    disk_sum = jnp.sum(matches * weighted[:, None], 0)
    disk_area = jnp.sum(matches * weight_sums[:, None], 0)
    disk_sum, disk_area = lax.psum((disk_sum, disk_area), ("gx", "gy"))
    disk_speed = disk_sum / jnp.maximum(disk_area, 1.0)
    thrust = -0.5 * thrust_coef * disk_speed * jnp.abs(disk_speed)
    row_thrust = jnp.sum(matches * thrust[None, :], 1)
    spread = (tile_weight * row_thrust[:, None]).reshape(-1)
    turbine_force = jnp.zeros((cells_dev,), jnp.float32).at[tile_cells.reshape(-1)].add(spread)
    laplace = neighbour_sum(extended) - 6.0 * fluctuation
    advect = (
        full_speed[0] * gradients[0] + full_speed[1] * gradients[1] + full_speed[2] * gradients[2]
    )
    tendency = viscosity * laplace - advect + closure.reshape(3, span_x, span_y, depth)
    tendency = tendency.at[0].add(turbine_force.reshape(span_x, span_y, depth))
    provisional = (fluctuation + step_dt * tendency).astype(jnp.bfloat16)
    velocity_new, force_field, cost_parts = project(provisional, target[0])
    force_grad = force_field.reshape(3, cells_dev)
    grad_weight_out = contract_cells(force_grad, hidden_two)
    grad_bias_out = jnp.sum(force_grad.astype(jnp.float32), 1)
    back_two = jnp.dot(weight_out.T, force_grad, preferred_element_type=jnp.float32)
    two_value = hidden_two.astype(jnp.float32)
    delta_two = (back_two * (1.0 - two_value * two_value)).astype(jnp.bfloat16)
    grad_bias_mid = jnp.sum(delta_two.astype(jnp.float32), 1)
    back_one = jnp.dot(weight_mid.T, delta_two, preferred_element_type=jnp.float32)
    one_value = hidden_one.astype(jnp.float32)
    delta_one = (back_one * (1.0 - one_value * one_value)).astype(jnp.bfloat16)
    grad_weight_in = contract_cells(delta_one, features)
    grad_bias_in = jnp.sum(delta_one.astype(jnp.float32), 1)
    grad_weight_mid = contract_cells(delta_two, hidden_one)
    devices = lax.axis_size("case") * lax.axis_size("gx") * lax.axis_size("gy")
    units = weight_mid.shape[0]
    small = jnp.concatenate(
        [
            grad_weight_in.reshape(-1),
            grad_bias_in,
            grad_bias_mid,
            grad_weight_out.reshape(-1),
            grad_bias_out,
            jnp.sum(cost_parts)[None],
        ]
    )
    small_count = small.shape[0]
    small = jnp.pad(small, (0, devices * 128 - small_count)).reshape(devices, 1, 128)
    parts = jnp.concatenate([grad_weight_mid.reshape(devices, -1, 128), small], 1)
    summed = reduce_all(parts)
    big = summed[:, :-1].reshape(units, units)
    small = summed[:, -1].reshape(-1)[:small_count]
    cost = small[-1]
    small = small[:-1]
    entry_total = units * units + small.shape[0]
    squares = jnp.sum(big * big) + jnp.sum(small * small)
    scale_rms = jnp.sqrt(squares / entry_total + epsilon_rms)
    big = big / scale_rms
    small = small / scale_rms
    bounds = np.cumsum([units * weight_in.shape[1], units, units, 3 * units])
    first, second, third, fourth, fifth = jnp.split(small, bounds)
    loss = cost / (3 * cells_dev * devices)
    return (
        velocity_new[None],
        loss,
        first.reshape(weight_in.shape),
        second,
        big,
        third,
        fourth.reshape(weight_out.shape),
        fifth,
        force_field[None],
    )


def solution(mesh):
    placed = (
        P("case", None, "gx", "gy", None),
        P("case", None, "gx", "gy", None),
        P(),
        P(),
        P(),
        P(),
        P(),
        P(),
        P(),
        P(("gx", "gy"), None),
        P(("gx", "gy")),
        P(("gx", "gy"), None),
    )
    return jax.shard_map(
        on_device,
        mesh=mesh,
        in_specs=placed,
        out_specs=(
            P("case", None, "gx", "gy", None),
            P(),
            P(),
            P(),
            P(),
            P(),
            P(),
            P(),
            P("case", None, "gx", "gy", None),
        ),
        check_vma=False,
    )
```

```python
import functools
import math

import jax
import jax.numpy as jnp
import numpy as np
from jax import lax
from jax.experimental import pallas as pl
from jax.experimental.pallas import tpu as pltpu
from jax.sharding import PartitionSpec as P

ITERS = 20
MESH = pl.DeviceIdType.MESH
HIGHEST = lax.Precision.HIGHEST
F32 = jnp.float32
BF16 = jnp.bfloat16

inflow = 1.0
step_dt = 0.4
viscosity = 0.1
epsilon_rms = 1e-06

ROWS = 24
LIVE = 18
SLOTS = 32
FIRST = 8
STEP = 2
CHANNELS = 16
FEATS = 12


def sines(count):
    index = np.arange(1, count + 1, dtype=np.float64)
    return math.sqrt(2.0 / (count + 1)) * np.sin(math.pi * np.outer(index, index) / (count + 1))


def cosines(count):
    return 2.0 * np.cos(math.pi * np.arange(1, count + 1, dtype=np.float64) / (count + 1))


def solve_tables(n_gx, n_gy, span_x, span_y, depth):
    nx, ny = n_gx * span_x, n_gy * span_y
    group = n_gx * n_gy
    modes = depth // group
    base_x, base_y = sines(nx), sines(ny)
    in_y = np.zeros((n_gy, modes, SLOTS, modes, ny))
    for gy in range(n_gy):
        for slot in range(FIRST - 1, FIRST + span_y + 1):
            y = gy * span_y + slot - FIRST
            if 0 <= y < ny:
                for mode in range(modes):
                    in_y[gy, mode, slot, mode] = base_y[y]
    in_y = in_y.reshape(n_gy * modes * SLOTS, modes * ny)
    in_x = np.zeros((nx, n_gx, ROWS))
    for gx in range(n_gx):
        for row in range(LIVE):
            x = gx * span_x + (row if row < span_x else (-1 if row == span_x else span_x))
            if 0 <= x < nx:
                in_x[:, gx, row] = base_x[x]
    in_x = in_x.reshape(nx, n_gx * ROWS)
    plane = np.tile((cosines(nx)[:, None] + cosines(ny)[None, :]) / 6.0, (1, modes))
    level = np.repeat((cosines(depth) / 6.0).reshape(modes, group).T, ny, axis=1)
    tables = (sines(depth), in_y, in_y.T, in_x, in_x.T, plane, level[:, None, :])
    return tuple(np.ascontiguousarray(table, dtype=np.float32) for table in tables)


def dot_full(left, right):
    return jnp.dot(left, right, precision=HIGHEST, preferred_element_type=jnp.float32)


def depth_difference(values):
    dim = values.ndim - 1
    depth = values.shape[dim]
    lane = lax.broadcasted_iota(jnp.int32, values.shape, dim)
    above = jnp.where(lane == depth - 1, 0.0, pltpu.roll(values, depth - 1, dim))
    below = jnp.where(lane == 0, 0.0, pltpu.roll(values, 1, dim))
    return above - below


def swap_groups(pieces, stride):
    count = len(pieces)
    lane = lax.broadcasted_iota(jnp.int32, pieces[0].shape, 1) // stride
    results = []
    for b in range(count):
        result = None
        for a in range(count):
            shift = ((a - b) * stride) % (count * stride)
            moved = pieces[a] if shift == 0 else pltpu.roll(pieces[a], shift, 1)
            result = moved if result is None else jnp.where(lane == a, moved, result)
        results.append(result)
    return results


def mm(left, right):
    return jnp.dot(left, right, preferred_element_type=F32)


def mm_cells(left, right):
    return lax.dot_general(left, right, (((1,), (1,)), ((), ())), preferred_element_type=F32)


def split_three(values):
    high = values.astype(BF16)
    rest = values - high.astype(F32)
    middle = rest.astype(BF16)
    low = (rest - middle.astype(F32)).astype(BF16)
    return high, middle, low


def column(row):
    return jnp.broadcast_to(row, (128, row.shape[1])).T[:, 0:1]


def step_kernel(
    sizes,
    v_ref,
    t_ref,
    weight_in,
    bias_in,
    weight_mid,
    bias_mid,
    weight_out,
    bias_out,
    thrust_coef,
    tile_cells,
    tile_turbine,
    tile_weight,
    base_z,
    in_y,
    out_y,
    in_x,
    out_x,
    plane,
    level,
    new_ref,
    loss_ref,
    step_in,
    step_bin,
    step_mid,
    step_bmid,
    step_out,
    step_bout,
    force_ref,
    rext,
    pext,
    vpad,
    tend,
    field,
    gain,
    features,
    one,
    two,
    stage,
    forces,
    result,
    w_one,
    w_out,
    w_mid_back,
    w_out_back,
    b_mid,
    coef,
    g_mid,
    g_out,
    g_in,
    small,
    halo_send,
    halo_x,
    halo_y,
    disk_send,
    disk_recv,
    send_a,
    recv_a,
    send_b,
    recv_b,
    recv_c,
    recv_d,
    cross,
    mine,
    halo_ssem,
    halo_rsem,
    send_sem,
    recv_sem,
    cross_ssem,
    cross_rsem,
):
    n_case, n_gx, n_gy = sizes
    case, gx, gy = lax.axis_index("case"), lax.axis_index("gx"), lax.axis_index("gy")
    group = n_gx * n_gy
    me = gy * n_gx + gx
    span_x, span_y, depth = v_ref.shape[2:]
    modes = depth // group
    units = weight_mid.shape[0]
    last = FIRST + span_y
    steps = span_x // STEP
    lines = STEP * span_y

    def device(index):
        return (case, lax.rem(index, n_gx), index // n_gx)

    for side in range(2):
        recv_a[side, :, span_x:, :] = jnp.zeros((group, ROWS - span_x, depth), F32)

    barrier = pltpu.get_barrier_semaphore()

    def greet(step, carry):
        pl.semaphore_signal(
            barrier,
            inc=1,
            device_id=device(lax.rem(me + step, group)),
            device_id_type=MESH,
        )
        return carry

    lax.fori_loop(1, group, greet, 0)
    for step in range(1, n_case):
        pl.semaphore_signal(
            barrier,
            inc=1,
            device_id=(lax.rem(case + step, n_case), gx, gy),
            device_id_type=MESH,
        )

    row_z = lax.broadcasted_iota(jnp.int32, (depth, 128), 0)
    row_xy = lax.broadcasted_iota(jnp.int32, (span_x * span_y, 128), 0)
    lane = lax.broadcasted_iota(jnp.int32, (1, 128), 1)
    tiles = tile_cells.shape[0]
    stream = v_ref[0, 0].reshape(span_x * span_y, depth)
    disk_sum = jnp.zeros((1, 128), F32)
    disk_area = jnp.zeros((1, 128), F32)
    for tile in range(tiles):
        cells = tile_cells[tile : tile + 1, :]
        weights = tile_weight[tile : tile + 1, :]
        pick_z = jnp.where(row_z == cells % depth, 1.0, 0.0).astype(BF16)
        levels = mm(stream, pick_z)
        sampled = jnp.sum(jnp.where(row_xy == cells // depth, levels, 0.0), 0, keepdims=True)
        weighted = jnp.sum(weights * (sampled + inflow), 1, keepdims=True)
        area = jnp.sum(weights, 1, keepdims=True)
        match = lane == tile_turbine[tile]
        disk_sum = disk_sum + jnp.where(match, weighted, 0.0)
        disk_area = disk_area + jnp.where(match, area, 0.0)
    disk_send[0:1, :] = disk_sum
    disk_send[1:2, :] = disk_area

    vpad[...] = jnp.zeros_like(vpad)
    for component in range(3):
        values = v_ref[0, component].astype(F32)
        vpad[component, 1 : span_x + 1, FIRST:last, :] = values
        halo_send[0, component] = values[:, 0, :].astype(BF16)
        halo_send[1, component] = values[:, span_y - 1, :].astype(BF16)

    w_one[...] = jnp.zeros_like(w_one)
    w_one[:, 0:FEATS] = weight_in[...].astype(F32)
    for place, part in enumerate(split_three(column(bias_in[...]))):
        w_one[:, FEATS + place : FEATS + place + 1] = part.astype(F32)
    w_out[...] = jnp.zeros_like(w_out)
    w_out[0:3, :] = weight_out[...].astype(F32)
    w_out_back[...] = w_out[...].T.astype(BF16)
    w_mid_back[...] = weight_mid[...].astype(F32).T.astype(BF16)
    b_mid[...] = column(bias_mid[...])
    coef[...] = jnp.zeros_like(coef)
    coef[0:1, 0 : thrust_coef.shape[1]] = thrust_coef[...]
    line_row = lax.broadcasted_iota(jnp.int32, stage.shape, 1)
    stage[...] = jnp.where((line_row >= FEATS) & (line_row < FEATS + 3), 1.0, 0.0)
    forces[...] = jnp.where(line_row == 3, 1.0, 0.0)

    ratio = plane[...] + level[me]
    total = jnp.ones_like(ratio)
    for _ in range(ITERS - 1):
        total = total * ratio + 1.0
    gain[...] = total * (-1.0 / 24.0)
    rext[...] = jnp.zeros_like(rext)

    pl.semaphore_wait(barrier, group - 1 + n_case - 1)

    copies = []
    for side, (source, place) in enumerate(((span_x - 1, 1), (0, n_gx - 1))):
        copies.append(
            pltpu.make_async_remote_copy(
                src_ref=v_ref.at[0, :, source],
                dst_ref=halo_x.at[side],
                send_sem=halo_ssem.at[side],
                recv_sem=halo_rsem.at[side],
                device_id=(case, lax.rem(gx + place, n_gx), gy),
                device_id_type=MESH,
            )
        )
    for side, (source, place) in enumerate(((1, 1), (0, n_gy - 1))):
        copies.append(
            pltpu.make_async_remote_copy(
                src_ref=halo_send.at[source],
                dst_ref=halo_y.at[side],
                send_sem=halo_ssem.at[2 + side],
                recv_sem=halo_rsem.at[2 + side],
                device_id=(case, gx, lax.rem(gy + place, n_gy)),
                device_id_type=MESH,
            )
        )
    for copy in copies:
        copy.start()

    def send_disk(step, carry):
        peer = lax.rem(me + step, group)
        pltpu.make_async_remote_copy(
            src_ref=disk_send,
            dst_ref=disk_recv.at[me],
            send_sem=send_sem.at[6],
            recv_sem=recv_sem.at[6],
            device_id=device(peer),
            device_id_type=MESH,
        ).start()
        return carry

    lax.fori_loop(1, group, send_disk, 0)
    disk_recv[me] = disk_send[...]

    for copy in copies:
        copy.wait()
    for component in range(3):
        for side, (row, inside) in enumerate(((0, gx > 0), (span_x + 1, gx < n_gx - 1))):
            values = halo_x[side, component].astype(F32)
            vpad[component, row, FIRST:last, :] = jnp.where(inside, values, 0.0)
        for side, (slot, inside) in enumerate(((FIRST - 1, gy > 0), (last, gy < n_gy - 1))):
            values = halo_y[side, component].astype(F32)
            vpad[component, 1 : span_x + 1, slot, :] = jnp.where(inside, values, 0.0)

    def forward(step, carry):
        base = step * STEP
        rows = pl.ds(base + 1, STEP)
        tendency = []
        speeds = []
        slopes = []
        for component in range(3):
            middle = vpad[component, rows, FIRST:last, :]
            above_x = vpad[component, pl.ds(base + 2, STEP), FIRST:last, :]
            below_x = vpad[component, pl.ds(base, STEP), FIRST:last, :]
            above_y = vpad[component, rows, FIRST + 1 : last + 1, :]
            below_y = vpad[component, rows, FIRST - 1 : last - 1, :]
            level_of = lax.broadcasted_iota(jnp.int32, middle.shape, 2)
            above_z = jnp.where(level_of == depth - 1, 0.0, pltpu.roll(middle, depth - 1, 2))
            below_z = jnp.where(level_of == 0, 0.0, pltpu.roll(middle, 1, 2))
            slopes.append(
                [
                    0.5 * (above_x - below_x),
                    0.5 * (above_y - below_y),
                    0.5 * (above_z - below_z),
                ]
            )
            around = above_x + below_x + above_y + below_y + above_z + below_z
            tendency.append(viscosity * (around - 6.0 * middle))
            speeds.append(middle)
        for component in range(3):
            for axis in range(3):
                stage[:, axis * 3 + component, :] = slopes[component][axis].reshape(lines, depth)
            stage[:, 9 + component, :] = speeds[component].reshape(lines, depth)
            advect = (
                (speeds[0] + inflow) * slopes[component][0]
                + speeds[1] * slopes[component][1]
                + speeds[2] * slopes[component][2]
            )
            tendency[component] = tendency[component] - advect
        for line in range(lines):
            features[step, :, line * depth : (line + 1) * depth] = stage[line].astype(BF16)
        inputs = features[step]
        hidden_one = jnp.tanh(mm(w_one[...].astype(BF16), inputs)).astype(BF16)
        one[step] = hidden_one
        hidden_two = jnp.tanh(mm(weight_mid[...], hidden_one) + b_mid[...]).astype(BF16)
        two[step] = hidden_two
        closure = mm(w_out[...].astype(BF16), hidden_two)
        for line in range(lines):
            result[line] = closure[0:8, line * depth : (line + 1) * depth]
        for component in range(3):
            added = result[:, component, :].reshape(STEP, span_y, depth) + bias_out[component]
            tend[component, pl.ds(base, STEP)] = tendency[component] + added
        return carry

    lax.fori_loop(0, steps, forward, 0)

    landed = disk_recv.at[pl.ds(0, group - 1)]
    pltpu.make_async_copy(landed, landed, recv_sem.at[6]).wait()
    pltpu.make_async_copy(landed, landed, send_sem.at[6]).wait()
    disks = jnp.sum(disk_recv[...], 0)
    disk_speed = disks[0:1, :] / jnp.maximum(disks[1:2, :], 1.0)
    thrust = -0.5 * coef[0:1, :] * disk_speed * jnp.abs(disk_speed)
    pushed = jnp.zeros((span_x * span_y, depth), F32)
    for tile in range(tiles):
        cells = tile_cells[tile : tile + 1, :]
        row_thrust = jnp.sum(
            jnp.where(lane == tile_turbine[tile], thrust, 0.0), 1, keepdims=True
        )
        spread = tile_weight[tile : tile + 1, :] * row_thrust
        pick_xy = jnp.where(row_xy == cells // depth, 1.0, 0.0).astype(BF16)
        placed = jnp.where(row_z == cells % depth, spread, 0.0)
        for part in split_three(placed):
            pushed = pushed + mm_cells(pick_xy, part)
    tend[0] = tend[0] + pushed.reshape(span_x, span_y, depth)
    for component in range(3):
        speed = vpad[component, 1 : span_x + 1, FIRST:last, :]
        provisional = (speed + step_dt * tend[component]).astype(BF16)
        tend[component] = provisional.astype(F32)

    def exchange(number, outgoing, incoming, same=False):
        def start(step, carry):
            peer = lax.rem(me + step, group)
            source = outgoing if same else outgoing.at[peer]
            pltpu.make_async_remote_copy(
                src_ref=source.at[pl.ds(0, LIVE)],
                dst_ref=incoming.at[me, pl.ds(0, LIVE)],
                send_sem=send_sem.at[number],
                recv_sem=recv_sem.at[number],
                device_id=device(peer),
                device_id_type=MESH,
            ).start()
            return carry

        lax.fori_loop(1, group, start, 0)
        if same:
            incoming[me, pl.ds(0, LIVE)] = outgoing[pl.ds(0, LIVE)]
        else:
            incoming[me, pl.ds(0, LIVE)] = outgoing[me, pl.ds(0, LIVE)]
        landed = incoming.at[pl.ds(0, group - 1), pl.ds(0, LIVE)]
        pltpu.make_async_copy(landed, landed, recv_sem.at[number]).wait()

    def sent(number):
        left = send_a.at[pl.ds(0, group - 1), pl.ds(0, LIVE)]
        pltpu.make_async_copy(left, left, send_sem.at[number]).wait()

    def solve(number, q_x, q_y, q_z):
        zero_x = jnp.zeros((1, span_y, depth), F32)
        inner = jnp.concatenate([q_x[1:], zero_x], 0) - jnp.concatenate([zero_x, q_x[:-1]], 0)
        inner = inner + depth_difference(q_z)
        wide = jnp.concatenate(
            [
                jnp.zeros((span_x, FIRST, depth), F32),
                q_y,
                jnp.zeros((span_x, SLOTS - last, depth), F32),
            ],
            1,
        )
        rext[0:span_x] = pltpu.roll(wide, SLOTS - 1, 1) - pltpu.roll(wide, 1, 1)
        rext[0:span_x, FIRST:last, :] = rext[0:span_x, FIRST:last, :] + inner
        rext[span_x, FIRST:last, :] = q_x[0]
        rext[span_x + 1, FIRST:last, :] = -q_x[span_x - 1]
        if number > 0:
            sent(2 * number - 2)
        for part in range(rext.shape[0] // modes):
            cells = rext[part * modes : (part + 1) * modes].reshape(modes * SLOTS, depth)
            turned = dot_full(cells, base_z[...]).T
            pieces = [turned[m * group : (m + 1) * group] for m in range(modes)]
            for inside, piece in enumerate(swap_groups(pieces, SLOTS)):
                if part * modes + inside < LIVE:
                    send_a[:, part * modes + inside, :] = piece
        arrived = recv_a.at[number]
        exchange(2 * number, send_a, arrived)
        along_y = None
        for block in range(n_gy):
            rows = arrived[block * n_gx : (block + 1) * n_gx].reshape(n_gx * ROWS, depth)
            part = dot_full(rows, in_y[block * depth : (block + 1) * depth, :])
            along_y = part if along_y is None else along_y + part
        spectrum = dot_full(in_x[...], along_y) * gain[...]
        back = dot_full(out_x[...], spectrum)
        if number > 0:
            sent(2 * number - 1)
        for block in range(n_gy):
            part = dot_full(back, out_y[:, block * depth : (block + 1) * depth])
            send_b[block * n_gx : (block + 1) * n_gx] = part.reshape(n_gx, ROWS, depth)
        arrived = recv_b.at[number]
        exchange(2 * number + 1, send_b, arrived)
        for part in range(pext.shape[0] // modes):
            pieces = [
                arrived[:, min(part * modes + inside, LIVE - 1), :] for inside in range(modes)
            ]
            turned = jnp.concatenate(swap_groups(pieces, SLOTS), 0).T
            pext[part * modes : (part + 1) * modes] = dot_full(turned, base_z[...]).reshape(
                modes, SLOTS, depth
            )

    def slope():
        middle = pext[0:span_x, FIRST:last, :]
        low = pext[span_x : span_x + 1, FIRST:last, :]
        high = pext[span_x + 1 : span_x + 2, FIRST:last, :]
        along_x = jnp.concatenate([middle[1:], high], 0) - jnp.concatenate([low, middle[:-1]], 0)
        along_y = (
            pext[0:span_x, FIRST + 1 : last + 1, :] - pext[0:span_x, FIRST - 1 : last - 1, :]
        )
        return along_x, along_y, depth_difference(middle)

    solve(0, tend[0], tend[1], tend[2])
    cost = jnp.zeros((1, depth), F32)
    for component, change in enumerate(slope()):
        updated = tend[component] - change
        new_ref[0, component] = updated.astype(BF16)
        mismatch = updated - t_ref[0, component].astype(F32)
        cost = cost + jnp.sum(
            (mismatch * mismatch).reshape(span_x * span_y, depth), 0, keepdims=True
        )
        field[component] = 2.0 * mismatch
    small[...] = jnp.zeros_like(small)
    small[43:44, :] = cost
    solve(1, field[0], field[1], field[2])
    for component, change in enumerate(slope()):
        force = (step_dt * (field[component] - change)).astype(BF16)
        force_ref[0, component] = force
        force = force.astype(F32)
        field[component] = force
        small[40 + component : 41 + component, :] = jnp.sum(
            force.reshape(span_x * span_y, depth), 0, keepdims=True
        )

    g_mid[...] = jnp.zeros_like(g_mid)
    g_out[...] = jnp.zeros_like(g_out)
    g_in[...] = jnp.zeros_like(g_in)

    def backward(step, carry):
        base = step * STEP
        for component in range(3):
            forces[:, component, :] = field[component, pl.ds(base, STEP)].reshape(lines, depth)
        force = jnp.concatenate([forces[line].astype(BF16) for line in range(lines)], 1)
        hidden_two = two[step]
        hidden_one = one[step]
        value = hidden_two.astype(F32)
        delta_two = (mm(w_out_back[...], force) * (1.0 - value * value)).astype(BF16)
        g_out[...] = g_out[...] + mm_cells(force, hidden_two)
        g_mid[0:units, :] = g_mid[0:units, :] + mm_cells(hidden_one, delta_two)
        g_mid[units:, :] = g_mid[units:, :] + mm_cells(force, delta_two)
        value = hidden_one.astype(F32)
        delta_one = (mm(w_mid_back[...], delta_two) * (1.0 - value * value)).astype(BF16)
        g_in[...] = g_in[...] + mm_cells(features[step], delta_one)
        return carry

    lax.fori_loop(0, steps, backward, 0)

    sent(2)
    for half in range(2):
        lanes = slice(half * 128, half * 128 + 128)
        small[half * CHANNELS : (half + 1) * CHANNELS, :] = g_in[:, lanes]
        small[32 + half : 33 + half, :] = g_mid[units + 3 : units + 4, lanes]
        small[34 + 3 * half : 37 + 3 * half, :] = g_out[0:3, lanes]
    middle = g_mid[0:units, :].T
    for owner in range(group):
        tile = middle[owner * 8 : (owner + 1) * 8, :]
        send_a[owner, 0:8, :] = tile[:, 0:128]
        send_a[owner, 8:16, :] = tile[:, 128:256]
        send_a[owner, 16:18, :] = small[2 * owner : 2 * owner + 2, :]
    exchange(4, send_a, recv_c)
    mine[...] = jnp.sum(recv_c[:, 0:LIVE, :], 0)
    copies = []
    for step in range(1, n_case):
        copies.append(
            pltpu.make_async_remote_copy(
                src_ref=mine,
                dst_ref=cross.at[step - 1],
                send_sem=cross_ssem.at[step - 1],
                recv_sem=cross_rsem.at[step - 1],
                device_id=(lax.rem(case + step, n_case), gx, gy),
                device_id_type=MESH,
            )
        )
    for copy in copies:
        copy.start()
    for copy in copies:
        copy.wait()
    places = []
    for source in range(n_case):
        step = lax.rem(case - source + n_case, n_case)
        there = cross[lax.max(step - 1, 0)]
        places.append(jnp.where(step == 0, mine[...], there))
    whole = places[0]
    for place in places[1:]:
        whole = whole + place
    sent(3)
    send_b[0, 0:LIVE, :] = whole
    exchange(5, send_b.at[0], recv_d, True)
    for owner in range(group):
        small[2 * owner : 2 * owner + 2, :] = recv_d[owner, 16:18, :]
    big = recv_d[:, 0:16, :].reshape(group * 16, 128)
    rest = small[...]
    bout = jnp.sum(rest[40:43], 1, keepdims=True)
    cost = jnp.sum(rest[43:44], 1, keepdims=True)
    row = lax.broadcasted_iota(jnp.int32, rest.shape, 0)
    inner_row = row % CHANNELS
    counted = ((row < 32) & (inner_row <= FEATS)) | ((row >= 32) & (row < 40))
    kept = jnp.where(counted, rest, 0.0)
    squares = jnp.sum(jnp.sum(big * big, 0, keepdims=True), 1, keepdims=True)
    squares = squares + jnp.sum(jnp.sum(kept * kept, 0, keepdims=True), 1, keepdims=True)
    squares = squares + jnp.sum(bout * bout, 0, keepdims=True)
    entries = units * FEATS + units + units * units + units + 3 * units + 3
    scale_rms = jnp.sqrt(squares / entries + epsilon_rms)
    for owner in range(group):
        step_mid[owner * 8 : (owner + 1) * 8, 0:128] = recv_d[owner, 0:8, :] / scale_rms
        step_mid[owner * 8 : (owner + 1) * 8, 128:256] = recv_d[owner, 8:16, :] / scale_rms
    scaled = rest / scale_rms
    for half in range(2):
        lanes = slice(half * 128, half * 128 + 128)
        block = scaled[half * CHANNELS : (half + 1) * CHANNELS, :]
        tall = jnp.concatenate([block, jnp.zeros((128 - CHANNELS, 128), F32)], 0).T
        step_in[lanes, :] = tall[:, 0:FEATS]
        step_bin[0:1, lanes] = block[FEATS : FEATS + 1, :]
        step_bmid[0:1, lanes] = scaled[32 + half : 33 + half, :]
        step_out[:, lanes] = scaled[34 + 3 * half : 37 + 3 * half, :]
    step_bout[...] = bout / scale_rms
    cells_all = 3 * n_case * group * span_x * span_y * depth
    loss_ref[...] = cost / cells_all
    sent(4)
    sent(5)


def on_device(
    velocity,
    target,
    weight_in,
    bias_in,
    weight_mid,
    bias_mid,
    weight_out,
    bias_out,
    thrust_coef,
    tile_cells,
    tile_turbine,
    tile_weight,
):
    sizes = tuple(lax.axis_size(axis) for axis in ("case", "gx", "gy"))
    n_case, n_gx, n_gy = sizes
    group = n_gx * n_gy
    _, _, span_x, span_y, depth = velocity.shape
    units = weight_mid.shape[0]
    tables = solve_tables(n_gx, n_gy, span_x, span_y, depth)
    vmem = pl.BlockSpec(memory_space=pltpu.VMEM)
    smem = pl.BlockSpec(memory_space=pltpu.SMEM)
    steps = span_x // STEP
    lines = STEP * span_y
    wide = lines * depth
    outs = pl.pallas_call(
        functools.partial(step_kernel, sizes),
        out_shape=(
            jax.ShapeDtypeStruct(velocity.shape, BF16),
            jax.ShapeDtypeStruct((1, 1), F32),
            jax.ShapeDtypeStruct((units, FEATS), F32),
            jax.ShapeDtypeStruct((1, units), F32),
            jax.ShapeDtypeStruct((units, units), F32),
            jax.ShapeDtypeStruct((1, units), F32),
            jax.ShapeDtypeStruct((3, units), F32),
            jax.ShapeDtypeStruct((3, 1), F32),
            jax.ShapeDtypeStruct(velocity.shape, BF16),
        ),
        in_specs=[vmem] * 7 + [smem, vmem, vmem, smem, vmem] + [vmem] * len(tables),
        out_specs=(vmem,) * 9,
        scratch_shapes=[
            pltpu.VMEM((span_x + 4, SLOTS, depth), F32),
            pltpu.VMEM((span_x + 4, SLOTS, depth), F32),
            pltpu.VMEM((3, span_x + 2, SLOTS, depth), F32),
            pltpu.VMEM((3, span_x, span_y, depth), F32),
            pltpu.VMEM((3, span_x, span_y, depth), F32),
            pltpu.VMEM(tables[5].shape, F32),
            pltpu.VMEM((steps, CHANNELS, wide), BF16),
            pltpu.VMEM((steps, units, wide), BF16),
            pltpu.VMEM((steps, units, wide), BF16),
            pltpu.VMEM((lines, CHANNELS, depth), F32),
            pltpu.VMEM((lines, CHANNELS, depth), F32),
            pltpu.VMEM((lines, 8, depth), F32),
            pltpu.VMEM((units, CHANNELS), F32),
            pltpu.VMEM((CHANNELS, units), F32),
            pltpu.VMEM((units, units), BF16),
            pltpu.VMEM((units, CHANNELS), BF16),
            pltpu.VMEM((units, 1), F32),
            pltpu.VMEM((8, 128), F32),
            pltpu.VMEM((units + CHANNELS, units), F32),
            pltpu.VMEM((CHANNELS, units), F32),
            pltpu.VMEM((CHANNELS, units), F32),
            pltpu.VMEM((2 * group, 128), F32),
            pltpu.VMEM((2, 3, span_x, depth), BF16),
            pltpu.VMEM((2, 3, span_y, depth), BF16),
            pltpu.VMEM((2, 3, span_x, depth), BF16),
            pltpu.VMEM((2, 128), F32),
            pltpu.VMEM((group, 2, 128), F32),
            pltpu.VMEM((group, ROWS, depth), F32),
            pltpu.VMEM((2, group, ROWS, depth), F32),
            pltpu.VMEM((group, ROWS, depth), F32),
            pltpu.VMEM((2, group, ROWS, depth), F32),
            pltpu.VMEM((group, ROWS, depth), F32),
            pltpu.VMEM((group, ROWS, depth), F32),
            pltpu.VMEM((n_case - 1, LIVE, 128), F32),
            pltpu.VMEM((LIVE, 128), F32),
            pltpu.SemaphoreType.DMA((4,)),
            pltpu.SemaphoreType.DMA((4,)),
            pltpu.SemaphoreType.DMA((7,)),
            pltpu.SemaphoreType.DMA((7,)),
            pltpu.SemaphoreType.DMA((n_case - 1,)),
            pltpu.SemaphoreType.DMA((n_case - 1,)),
        ],
        compiler_params=pltpu.CompilerParams(
            collective_id=0, has_side_effects=True, vmem_limit_bytes=60 * 1024 * 1024
        ),
        name="flow_step",
    )(
        velocity,
        target,
        weight_in,
        bias_in[None, :],
        weight_mid,
        bias_mid[None, :],
        weight_out,
        bias_out,
        thrust_coef[None, :],
        tile_cells,
        tile_turbine,
        tile_weight,
        *tables,
    )
    new, loss, step_in, step_bin, step_mid, step_bmid, step_out, step_bout, force = outs
    return (
        new,
        loss[0, 0],
        step_in,
        step_bin[0],
        step_mid,
        step_bmid[0],
        step_out,
        step_bout[:, 0],
        force,
    )


def solution(mesh):
    placed = (
        P("case", None, "gx", "gy", None),
        P("case", None, "gx", "gy", None),
        P(),
        P(),
        P(),
        P(),
        P(),
        P(),
        P(),
        P(("gx", "gy"), None),
        P(("gx", "gy")),
        P(("gx", "gy"), None),
    )
    return jax.shard_map(
        on_device,
        mesh=mesh,
        in_specs=placed,
        out_specs=(
            P("case", None, "gx", "gy", None),
            P(),
            P(),
            P(),
            P(),
            P(),
            P(),
            P(),
            P("case", None, "gx", "gy", None),
        ),
        check_vma=False,
    )
```

```python
import functools
import math

import jax
import jax.numpy as jnp
import numpy as np
from jax import lax
from jax.experimental import pallas as pl
from jax.experimental.pallas import tpu as pltpu
from jax.sharding import PartitionSpec as P

ITERS = 20
MESH = pl.DeviceIdType.MESH
F32 = jnp.float32
BF16 = jnp.bfloat16

inflow = 1.0
step_dt = 0.4
viscosity = 0.1
epsilon_rms = 1e-06

ROWS = 24
LIVE = 18
SLOTS = 32
FIRST = 8
STEP = 2
CHANNELS = 16
FEATS = 12


def sines(count):
    index = np.arange(1, count + 1, dtype=np.float64)
    return math.sqrt(2.0 / (count + 1)) * np.sin(math.pi * np.outer(index, index) / (count + 1))


def cosines(count):
    return 2.0 * np.cos(math.pi * np.arange(1, count + 1, dtype=np.float64) / (count + 1))


def solve_tables(n_gx, n_gy, span_x, span_y, depth):
    nx, ny = n_gx * span_x, n_gy * span_y
    group = n_gx * n_gy
    modes = depth // group
    base_x, base_y = sines(nx), sines(ny)
    in_y = np.zeros((n_gy, modes, SLOTS, modes, ny))
    for gy in range(n_gy):
        for slot in range(FIRST - 1, FIRST + span_y + 1):
            y = gy * span_y + slot - FIRST
            if 0 <= y < ny:
                for mode in range(modes):
                    in_y[gy, mode, slot, mode] = base_y[y]
    in_y = in_y.reshape(n_gy * modes * SLOTS, modes * ny)
    in_x = np.zeros((nx, n_gx, ROWS))
    for gx in range(n_gx):
        for row in range(LIVE):
            x = gx * span_x + (row if row < span_x else (-1 if row == span_x else span_x))
            if 0 <= x < nx:
                in_x[:, gx, row] = base_x[x]
    in_x = in_x.reshape(nx, n_gx * ROWS)
    plane = np.tile((cosines(nx)[:, None] + cosines(ny)[None, :]) / 6.0, (1, modes))
    level = np.repeat((cosines(depth) / 6.0).reshape(modes, group).T, ny, axis=1)
    tables = (sines(depth), in_y, in_y.T, in_x, in_x.T, plane, level[:, None, :])
    return tuple(np.ascontiguousarray(table, dtype=np.float32) for table in tables)


def split_two(values):
    high = values.astype(BF16)
    return high, (values - high.astype(F32)).astype(BF16)


def dot_full(left, right):
    left_high, left_low = split_two(left)
    right_high, right_low = split_two(right)
    return (
        jnp.dot(left_low, right_high, preferred_element_type=F32)
        + jnp.dot(left_high, right_low, preferred_element_type=F32)
    ) + jnp.dot(left_high, right_high, preferred_element_type=F32)


def depth_difference(values):
    dim = values.ndim - 1
    depth = values.shape[dim]
    lane = lax.broadcasted_iota(jnp.int32, values.shape, dim)
    above = jnp.where(lane == depth - 1, 0.0, pltpu.roll(values, depth - 1, dim))
    below = jnp.where(lane == 0, 0.0, pltpu.roll(values, 1, dim))
    return above - below


def swap_groups(pieces, stride):
    count = len(pieces)
    lane = lax.broadcasted_iota(jnp.int32, pieces[0].shape, 1) // stride
    results = []
    for b in range(count):
        result = None
        for a in range(count):
            shift = ((a - b) * stride) % (count * stride)
            moved = pieces[a] if shift == 0 else pltpu.roll(pieces[a], shift, 1)
            result = moved if result is None else jnp.where(lane == a, moved, result)
        results.append(result)
    return results


def mm(left, right):
    return jnp.dot(left, right, preferred_element_type=F32)


def mm_cells(left, right):
    return lax.dot_general(left, right, (((1,), (1,)), ((), ())), preferred_element_type=F32)


def split_three(values):
    high = values.astype(BF16)
    rest = values - high.astype(F32)
    middle = rest.astype(BF16)
    low = (rest - middle.astype(F32)).astype(BF16)
    return high, middle, low


def column(row):
    return jnp.broadcast_to(row, (128, row.shape[1])).T[:, 0:1]


def step_kernel(
    sizes,
    v_ref,
    t_ref,
    weight_in,
    bias_in,
    weight_mid,
    bias_mid,
    weight_out,
    bias_out,
    thrust_coef,
    tile_cells,
    tile_turbine,
    tile_weight,
    base_z,
    in_y,
    out_y,
    in_x,
    out_x,
    plane,
    level,
    new_ref,
    loss_ref,
    step_in,
    step_bin,
    step_mid,
    step_bmid,
    step_out,
    step_bout,
    force_ref,
    rext,
    pext,
    vpad,
    tend,
    field,
    gain,
    features,
    one,
    two,
    stage,
    forces,
    result,
    w_one,
    w_out,
    w_mid_back,
    w_out_back,
    b_mid,
    coef,
    g_mid,
    g_out,
    g_in,
    g_bias,
    columns,
    small,
    halo_send,
    halo_x,
    halo_y,
    disk_send,
    disk_recv,
    send_a,
    recv_a,
    send_b,
    recv_b,
    recv_c,
    recv_d,
    cross,
    mine,
    halo_ssem,
    halo_rsem,
    send_sem,
    recv_sem,
    cross_ssem,
    cross_rsem,
):
    n_case, n_gx, n_gy = sizes
    case, gx, gy = lax.axis_index("case"), lax.axis_index("gx"), lax.axis_index("gy")
    group = n_gx * n_gy
    me = gy * n_gx + gx
    span_x, span_y, depth = v_ref.shape[2:]
    modes = depth // group
    units = weight_mid.shape[0]
    last = FIRST + span_y
    steps = span_x // STEP
    lines = STEP * span_y

    def device(index):
        return (case, lax.rem(index, n_gx), index // n_gx)

    for side in range(2):
        recv_a[side, :, span_x:, :] = jnp.zeros((group, ROWS - span_x, depth), F32)

    barrier = pltpu.get_barrier_semaphore()

    def greet(step, carry):
        pl.semaphore_signal(
            barrier,
            inc=1,
            device_id=device(lax.rem(me + step, group)),
            device_id_type=MESH,
        )
        return carry

    lax.fori_loop(1, group, greet, 0)
    for step in range(1, n_case):
        pl.semaphore_signal(
            barrier,
            inc=1,
            device_id=(lax.rem(case + step, n_case), gx, gy),
            device_id_type=MESH,
        )

    row_z = lax.broadcasted_iota(jnp.int32, (depth, 128), 0)
    row_xy = lax.broadcasted_iota(jnp.int32, (span_x * span_y, 128), 0)
    lane = lax.broadcasted_iota(jnp.int32, (1, 128), 1)
    tiles = tile_cells.shape[0]
    stream = v_ref[0, 0].reshape(span_x * span_y, depth)
    disk_sum = jnp.zeros((1, 128), F32)
    disk_area = jnp.zeros((1, 128), F32)
    for tile in range(tiles):
        cells = tile_cells[tile : tile + 1, :]
        weights = tile_weight[tile : tile + 1, :]
        pick_z = jnp.where(row_z == cells % depth, 1.0, 0.0).astype(BF16)
        levels = mm(stream, pick_z)
        sampled = jnp.sum(jnp.where(row_xy == cells // depth, levels, 0.0), 0, keepdims=True)
        weighted = jnp.sum(weights * (sampled + inflow), 1, keepdims=True)
        area = jnp.sum(weights, 1, keepdims=True)
        match = lane == tile_turbine[tile]
        disk_sum = disk_sum + jnp.where(match, weighted, 0.0)
        disk_area = disk_area + jnp.where(match, area, 0.0)
    disk_send[0:1, :] = disk_sum
    disk_send[1:2, :] = disk_area

    vpad[...] = jnp.zeros_like(vpad)
    for component in range(3):
        values = v_ref[0, component].astype(F32)
        vpad[component, 1 : span_x + 1, FIRST:last, :] = values
        halo_send[0, component] = values[:, 0, :].astype(BF16)
        halo_send[1, component] = values[:, span_y - 1, :].astype(BF16)

    stack = [weight_in[...].astype(F32)] + [
        part.astype(F32) for part in split_three(bias_in[...])
    ]
    stack.append(jnp.zeros((CHANNELS - FEATS - 3, units), F32))
    w_one[...] = jnp.concatenate(stack, 0).T.astype(BF16)
    w_out[...] = jnp.zeros_like(w_out)
    w_out[0:3, :] = weight_out[...].astype(F32)
    w_out_back[...] = w_out[...].T.astype(BF16)
    w_mid_back[...] = weight_mid[...].astype(F32).T.astype(BF16)
    b_mid[...] = column(bias_mid[...])
    coef[...] = jnp.zeros_like(coef)
    coef[0:1, 0 : thrust_coef.shape[1]] = thrust_coef[...]
    line_row = lax.broadcasted_iota(jnp.int32, stage.shape, 1)
    stage[...] = jnp.where((line_row >= FEATS) & (line_row < FEATS + 3), 1.0, 0.0)
    forces[...] = jnp.zeros_like(forces)

    ratio = plane[...] + level[me]
    total = jnp.ones_like(ratio)
    for _ in range(ITERS - 1):
        total = total * ratio + 1.0
    gain[...] = total * (-1.0 / 24.0)
    rext[...] = jnp.zeros_like(rext)

    pl.semaphore_wait(barrier, group - 1 + n_case - 1)

    copies = []
    for side, (source, place) in enumerate(((span_x - 1, 1), (0, n_gx - 1))):
        copies.append(
            pltpu.make_async_remote_copy(
                src_ref=v_ref.at[0, :, source],
                dst_ref=halo_x.at[side],
                send_sem=halo_ssem.at[side],
                recv_sem=halo_rsem.at[side],
                device_id=(case, lax.rem(gx + place, n_gx), gy),
                device_id_type=MESH,
            )
        )
    for side, (source, place) in enumerate(((1, 1), (0, n_gy - 1))):
        copies.append(
            pltpu.make_async_remote_copy(
                src_ref=halo_send.at[source],
                dst_ref=halo_y.at[side],
                send_sem=halo_ssem.at[2 + side],
                recv_sem=halo_rsem.at[2 + side],
                device_id=(case, gx, lax.rem(gy + place, n_gy)),
                device_id_type=MESH,
            )
        )
    for copy in copies:
        copy.start()

    def send_disk(step, carry):
        peer = lax.rem(me + step, group)
        pltpu.make_async_remote_copy(
            src_ref=disk_send,
            dst_ref=disk_recv.at[me],
            send_sem=send_sem.at[6],
            recv_sem=recv_sem.at[6],
            device_id=device(peer),
            device_id_type=MESH,
        ).start()
        return carry

    lax.fori_loop(1, group, send_disk, 0)
    disk_recv[me] = disk_send[...]

    for copy in copies:
        copy.wait()
    for component in range(3):
        for side, (row, inside) in enumerate(((0, gx > 0), (span_x + 1, gx < n_gx - 1))):
            values = halo_x[side, component].astype(F32)
            vpad[component, row, FIRST:last, :] = jnp.where(inside, values, 0.0)
        for side, (slot, inside) in enumerate(((FIRST - 1, gy > 0), (last, gy < n_gy - 1))):
            values = halo_y[side, component].astype(F32)
            vpad[component, 1 : span_x + 1, slot, :] = jnp.where(inside, values, 0.0)

    def forward(step, carry):
        base = step * STEP
        rows = pl.ds(base + 1, STEP)
        tendency = []
        speeds = []
        slopes = []
        for component in range(3):
            middle = vpad[component, rows, FIRST:last, :]
            above_x = vpad[component, pl.ds(base + 2, STEP), FIRST:last, :]
            below_x = vpad[component, pl.ds(base, STEP), FIRST:last, :]
            above_y = vpad[component, rows, FIRST + 1 : last + 1, :]
            below_y = vpad[component, rows, FIRST - 1 : last - 1, :]
            level_of = lax.broadcasted_iota(jnp.int32, middle.shape, 2)
            above_z = jnp.where(level_of == depth - 1, 0.0, pltpu.roll(middle, depth - 1, 2))
            below_z = jnp.where(level_of == 0, 0.0, pltpu.roll(middle, 1, 2))
            slopes.append(
                [
                    0.5 * (above_x - below_x),
                    0.5 * (above_y - below_y),
                    0.5 * (above_z - below_z),
                ]
            )
            around = above_x + below_x + above_y + below_y + above_z + below_z
            tendency.append(viscosity * (around - 6.0 * middle))
            speeds.append(middle)
        for component in range(3):
            for axis in range(3):
                stage[:, axis * 3 + component, :] = slopes[component][axis].reshape(lines, depth)
            stage[:, 9 + component, :] = speeds[component].reshape(lines, depth)
            advect = (
                (speeds[0] + inflow) * slopes[component][0]
                + speeds[1] * slopes[component][1]
                + speeds[2] * slopes[component][2]
            )
            tendency[component] = tendency[component] - advect
        for line in range(lines):
            features[step, :, line * depth : (line + 1) * depth] = stage[line].astype(BF16)
        inputs = features[step]
        hidden_one = jnp.tanh(mm(w_one[...], inputs)).astype(BF16)
        one[step] = hidden_one
        hidden_two = jnp.tanh(mm(weight_mid[...], hidden_one) + b_mid[...]).astype(BF16)
        two[step] = hidden_two
        closure = mm(w_out[...].astype(BF16), hidden_two)
        for line in range(lines):
            result[line] = closure[0:8, line * depth : (line + 1) * depth]
        for component in range(3):
            added = result[:, component, :].reshape(STEP, span_y, depth) + bias_out[component]
            tend[component, pl.ds(base, STEP)] = tendency[component] + added
        return carry

    lax.fori_loop(0, steps, forward, 0)

    landed = disk_recv.at[pl.ds(0, group - 1)]
    pltpu.make_async_copy(landed, landed, recv_sem.at[6]).wait()
    pltpu.make_async_copy(landed, landed, send_sem.at[6]).wait()
    disks = jnp.sum(disk_recv[...], 0)
    disk_speed = disks[0:1, :] / jnp.maximum(disks[1:2, :], 1.0)
    thrust = -0.5 * coef[0:1, :] * disk_speed * jnp.abs(disk_speed)
    pushed = jnp.zeros((span_x * span_y, depth), F32)
    for tile in range(tiles):
        cells = tile_cells[tile : tile + 1, :]
        row_thrust = jnp.sum(
            jnp.where(lane == tile_turbine[tile], thrust, 0.0), 1, keepdims=True
        )
        spread = tile_weight[tile : tile + 1, :] * row_thrust
        pick_xy = jnp.where(row_xy == cells // depth, 1.0, 0.0).astype(BF16)
        placed = jnp.where(row_z == cells % depth, spread, 0.0)
        for part in split_three(placed):
            pushed = pushed + mm_cells(pick_xy, part)
    tend[0] = tend[0] + pushed.reshape(span_x, span_y, depth)
    for component in range(3):
        speed = vpad[component, 1 : span_x + 1, FIRST:last, :]
        provisional = (speed + step_dt * tend[component]).astype(BF16)
        tend[component] = provisional.astype(F32)

    def exchange(number, outgoing, incoming, same=False):
        def start(step, carry):
            peer = lax.rem(me + step, group)
            source = outgoing if same else outgoing.at[peer]
            pltpu.make_async_remote_copy(
                src_ref=source.at[pl.ds(0, LIVE)],
                dst_ref=incoming.at[me, pl.ds(0, LIVE)],
                send_sem=send_sem.at[number],
                recv_sem=recv_sem.at[number],
                device_id=device(peer),
                device_id_type=MESH,
            ).start()
            return carry

        lax.fori_loop(1, group, start, 0)
        if same:
            incoming[me, pl.ds(0, LIVE)] = outgoing[pl.ds(0, LIVE)]
        else:
            incoming[me, pl.ds(0, LIVE)] = outgoing[me, pl.ds(0, LIVE)]
        landed = incoming.at[pl.ds(0, group - 1), pl.ds(0, LIVE)]
        pltpu.make_async_copy(landed, landed, recv_sem.at[number]).wait()

    def sent(number):
        left = send_a.at[pl.ds(0, group - 1), pl.ds(0, LIVE)]
        pltpu.make_async_copy(left, left, send_sem.at[number]).wait()

    def solve(number, q_x, q_y, q_z):
        zero_x = jnp.zeros((1, span_y, depth), F32)
        inner = jnp.concatenate([q_x[1:], zero_x], 0) - jnp.concatenate([zero_x, q_x[:-1]], 0)
        inner = inner + depth_difference(q_z)
        wide = jnp.concatenate(
            [
                jnp.zeros((span_x, FIRST, depth), F32),
                q_y,
                jnp.zeros((span_x, SLOTS - last, depth), F32),
            ],
            1,
        )
        rext[0:span_x] = pltpu.roll(wide, SLOTS - 1, 1) - pltpu.roll(wide, 1, 1)
        rext[0:span_x, FIRST:last, :] = rext[0:span_x, FIRST:last, :] + inner
        rext[span_x, FIRST:last, :] = q_x[0]
        rext[span_x + 1, FIRST:last, :] = -q_x[span_x - 1]
        if number > 0:
            sent(2 * number - 2)
        for part in range(rext.shape[0] // modes):
            cells = rext[part * modes : (part + 1) * modes].reshape(modes * SLOTS, depth)
            turned = dot_full(cells, base_z[...]).T
            pieces = [turned[m * group : (m + 1) * group] for m in range(modes)]
            for inside, piece in enumerate(swap_groups(pieces, SLOTS)):
                if part * modes + inside < LIVE:
                    send_a[:, part * modes + inside, :] = piece
        arrived = recv_a.at[number]
        exchange(2 * number, send_a, arrived)
        along_y = None
        for block in range(n_gy):
            rows = arrived[block * n_gx : (block + 1) * n_gx].reshape(n_gx * ROWS, depth)
            part = dot_full(rows, in_y[block * depth : (block + 1) * depth, :])
            along_y = part if along_y is None else along_y + part
        spectrum = dot_full(in_x[...], along_y) * gain[...]
        back = dot_full(out_x[...], spectrum)
        if number > 0:
            sent(2 * number - 1)
        arrived = recv_b.at[number]
        for block in range(n_gy):
            part = dot_full(back, out_y[:, block * depth : (block + 1) * depth])
            send_b[block * n_gx : (block + 1) * n_gx] = part.reshape(n_gx, ROWS, depth)
        exchange(2 * number + 1, send_b, arrived)
        for part in range(pext.shape[0] // modes):
            pieces = [
                arrived[:, min(part * modes + inside, LIVE - 1), :] for inside in range(modes)
            ]
            turned = jnp.concatenate(swap_groups(pieces, SLOTS), 0).T
            pext[part * modes : (part + 1) * modes] = dot_full(turned, base_z[...]).reshape(
                modes, SLOTS, depth
            )

    def slope():
        middle = pext[0:span_x, FIRST:last, :]
        low = pext[span_x : span_x + 1, FIRST:last, :]
        high = pext[span_x + 1 : span_x + 2, FIRST:last, :]
        along_x = jnp.concatenate([middle[1:], high], 0) - jnp.concatenate([low, middle[:-1]], 0)
        along_y = (
            pext[0:span_x, FIRST + 1 : last + 1, :] - pext[0:span_x, FIRST - 1 : last - 1, :]
        )
        return along_x, along_y, depth_difference(middle)

    solve(0, tend[0], tend[1], tend[2])
    cost = jnp.zeros((1, depth), F32)
    for component, change in enumerate(slope()):
        updated = tend[component] - change
        new_ref[0, component] = updated.astype(BF16)
        mismatch = updated - t_ref[0, component].astype(F32)
        cost = cost + jnp.sum(
            (mismatch * mismatch).reshape(span_x * span_y, depth), 0, keepdims=True
        )
        field[component] = 2.0 * mismatch
    small[...] = jnp.zeros_like(small)
    small[43:44, :] = cost
    solve(1, field[0], field[1], field[2])
    for component, change in enumerate(slope()):
        force = (step_dt * (field[component] - change)).astype(BF16)
        force_ref[0, component] = force
        force = force.astype(F32)
        field[component] = force
        small[40 + component : 41 + component, :] = jnp.sum(
            force.reshape(span_x * span_y, depth), 0, keepdims=True
        )

    g_mid[...] = jnp.zeros_like(g_mid)
    g_out[...] = jnp.zeros_like(g_out)
    g_in[...] = jnp.zeros_like(g_in)
    g_bias[...] = jnp.zeros_like(g_bias)

    share = 2 * CHANNELS
    packed = depth // share
    own_lane = lax.broadcasted_iota(jnp.int32, (depth, depth), 1) // share

    def backward(step, carry):
        base = step * STEP
        for component in range(3):
            forces[:, component, :] = field[component, pl.ds(base, STEP)].reshape(lines, depth)
        parts = []
        for first in range(0, lines, packed):
            rows = []
            for line in range(first, first + packed):
                parts.append(forces[line].astype(BF16))
                rows.append(forces[line])
                rows.append(features[step, :, line * depth : (line + 1) * depth].astype(F32))
            turned = jnp.concatenate(rows, 0).T
            for place in range(packed):
                line = first + place
                columns[line * depth : (line + 1) * depth, :] = jnp.where(
                    own_lane == place, turned, 0.0
                ).astype(BF16)
        force = jnp.concatenate(parts, 1)
        hidden_two = two[step]
        hidden_one = one[step]
        value = hidden_two.astype(F32)
        delta_two = (mm(w_out_back[...], force) * (1.0 - value * value)).astype(BF16)
        g_out[...] = g_out[...] + mm(hidden_two, columns[...])
        g_mid[...] = g_mid[...] + mm_cells(hidden_one, delta_two)
        tall = g_bias[...]
        for line in range(lines):
            tall = tall + delta_two[:, line * depth : (line + 1) * depth].astype(F32)
        g_bias[...] = tall
        value = hidden_one.astype(F32)
        delta_one = (mm(w_mid_back[...], delta_two) * (1.0 - value * value)).astype(BF16)
        g_in[...] = g_in[...] + mm(delta_one, columns[...])
        return carry

    lax.fori_loop(0, steps, backward, 0)

    sent(2)
    def folded(sums):
        rows = sums.T
        total = rows[0:share]
        for place in range(1, packed):
            total = total + rows[place * share : (place + 1) * share]
        return total

    for_in = folded(g_in[...])[CHANNELS:share]
    for_out = folded(g_out[...])[0:CHANNELS]
    for_bias = jnp.sum(g_bias[...].T, 0, keepdims=True)
    for half in range(2):
        lanes = slice(half * 128, half * 128 + 128)
        small[half * CHANNELS : (half + 1) * CHANNELS, :] = for_in[:, lanes]
        small[32 + half : 33 + half, :] = for_bias[:, lanes]
        small[34 + 3 * half : 37 + 3 * half, :] = for_out[0:3, lanes]
    middle = g_mid[...].T
    for owner in range(group):
        tile = middle[owner * 8 : (owner + 1) * 8, :]
        send_a[owner, 0:8, :] = tile[:, 0:128]
        send_a[owner, 8:16, :] = tile[:, 128:256]
        send_a[owner, 16:18, :] = small[2 * owner : 2 * owner + 2, :]
    exchange(4, send_a, recv_c)
    mine[...] = jnp.sum(recv_c[:, 0:LIVE, :], 0)
    copies = []
    for step in range(1, n_case):
        copies.append(
            pltpu.make_async_remote_copy(
                src_ref=mine,
                dst_ref=cross.at[step - 1],
                send_sem=cross_ssem.at[step - 1],
                recv_sem=cross_rsem.at[step - 1],
                device_id=(lax.rem(case + step, n_case), gx, gy),
                device_id_type=MESH,
            )
        )
    for copy in copies:
        copy.start()
    for copy in copies:
        copy.wait()
    places = []
    for source in range(n_case):
        step = lax.rem(case - source + n_case, n_case)
        there = cross[lax.max(step - 1, 0)]
        places.append(jnp.where(step == 0, mine[...], there))
    whole = places[0]
    for place in places[1:]:
        whole = whole + place
    sent(3)
    send_b[0, 0:LIVE, :] = whole
    exchange(5, send_b.at[0], recv_d, True)
    for owner in range(group):
        small[2 * owner : 2 * owner + 2, :] = recv_d[owner, 16:18, :]
    big = recv_d[:, 0:16, :].reshape(group * 16, 128)
    rest = small[...]
    bout = jnp.sum(rest[40:43], 1, keepdims=True)
    cost = jnp.sum(rest[43:44], 1, keepdims=True)
    row = lax.broadcasted_iota(jnp.int32, rest.shape, 0)
    inner_row = row % CHANNELS
    counted = ((row < 32) & (inner_row <= FEATS)) | ((row >= 32) & (row < 40))
    kept = jnp.where(counted, rest, 0.0)
    squares = jnp.sum(jnp.sum(big * big, 0, keepdims=True), 1, keepdims=True)
    squares = squares + jnp.sum(jnp.sum(kept * kept, 0, keepdims=True), 1, keepdims=True)
    squares = squares + jnp.sum(bout * bout, 0, keepdims=True)
    entries = units * FEATS + units + units * units + units + 3 * units + 3
    scale_rms = jnp.sqrt(squares / entries + epsilon_rms)
    for owner in range(group):
        step_mid[owner * 8 : (owner + 1) * 8, 0:128] = recv_d[owner, 0:8, :] / scale_rms
        step_mid[owner * 8 : (owner + 1) * 8, 128:256] = recv_d[owner, 8:16, :] / scale_rms
    scaled = rest / scale_rms
    for half in range(2):
        lanes = slice(half * 128, half * 128 + 128)
        block = scaled[half * CHANNELS : (half + 1) * CHANNELS, :]
        step_in[:, lanes] = block[0:FEATS, :]
        step_bin[0:1, lanes] = block[FEATS : FEATS + 1, :]
        step_bmid[0:1, lanes] = scaled[32 + half : 33 + half, :]
        step_out[:, lanes] = scaled[34 + 3 * half : 37 + 3 * half, :]
    diagonal = lax.broadcasted_iota(jnp.int32, (3, 128), 0) == lax.broadcasted_iota(
        jnp.int32, (3, 128), 1
    )
    flat = jnp.sum(jnp.where(diagonal, bout / scale_rms, 0.0), 0, keepdims=True)
    step_bout[...] = flat[:, 0:3]
    cells_all = 3 * n_case * group * span_x * span_y * depth
    loss_ref[...] = cost / cells_all
    sent(4)
    sent(5)


def hand_over(*refs):
    count = len(refs) // 2
    for source, target in zip(refs[:count], refs[count:]):
        target[...] = source[...]


def on_device(
    velocity,
    target,
    weight_in,
    bias_in,
    weight_mid,
    bias_mid,
    weight_out,
    bias_out,
    thrust_coef,
    tile_cells,
    tile_turbine,
    tile_weight,
):
    sizes = tuple(lax.axis_size(axis) for axis in ("case", "gx", "gy"))
    n_case, n_gx, n_gy = sizes
    group = n_gx * n_gy
    _, _, span_x, span_y, depth = velocity.shape
    units = weight_mid.shape[0]
    tables = solve_tables(n_gx, n_gy, span_x, span_y, depth)
    vmem = pl.BlockSpec(memory_space=pltpu.VMEM)
    smem = pl.BlockSpec(memory_space=pltpu.SMEM)
    steps = span_x // STEP
    lines = STEP * span_y
    wide = lines * depth
    outs = pl.pallas_call(
        functools.partial(step_kernel, sizes),
        out_shape=(
            jax.ShapeDtypeStruct(velocity.shape, BF16),
            jax.ShapeDtypeStruct((1, 1), F32),
            jax.ShapeDtypeStruct((FEATS, units), F32),
            jax.ShapeDtypeStruct((1, units), F32),
            jax.ShapeDtypeStruct((units, units), F32),
            jax.ShapeDtypeStruct((1, units), F32),
            jax.ShapeDtypeStruct((3, units), F32),
            jax.ShapeDtypeStruct((1, 3), F32),
            jax.ShapeDtypeStruct(velocity.shape, BF16),
        ),
        in_specs=[vmem] * 7 + [smem, vmem, vmem, smem, vmem] + [vmem] * len(tables),
        out_specs=(vmem,) * 9,
        scratch_shapes=[
            pltpu.VMEM((span_x + 4, SLOTS, depth), F32),
            pltpu.VMEM((span_x + 4, SLOTS, depth), F32),
            pltpu.VMEM((3, span_x + 2, SLOTS, depth), F32),
            pltpu.VMEM((3, span_x, span_y, depth), F32),
            pltpu.VMEM((3, span_x, span_y, depth), F32),
            pltpu.VMEM(tables[5].shape, F32),
            pltpu.VMEM((steps, CHANNELS, wide), BF16),
            pltpu.VMEM((steps, units, wide), BF16),
            pltpu.VMEM((steps, units, wide), BF16),
            pltpu.VMEM((lines, CHANNELS, depth), F32),
            pltpu.VMEM((lines, CHANNELS, depth), F32),
            pltpu.VMEM((lines, 8, depth), F32),
            pltpu.VMEM((units, CHANNELS), BF16),
            pltpu.VMEM((CHANNELS, units), F32),
            pltpu.VMEM((units, units), BF16),
            pltpu.VMEM((units, CHANNELS), BF16),
            pltpu.VMEM((units, 1), F32),
            pltpu.VMEM((8, 128), F32),
            pltpu.VMEM((units, units), F32),
            pltpu.VMEM((units, depth), F32),
            pltpu.VMEM((units, depth), F32),
            pltpu.VMEM((units, depth), F32),
            pltpu.VMEM((wide, depth), BF16),
            pltpu.VMEM((2 * group, 128), F32),
            pltpu.VMEM((2, 3, span_x, depth), BF16),
            pltpu.VMEM((2, 3, span_y, depth), BF16),
            pltpu.VMEM((2, 3, span_x, depth), BF16),
            pltpu.VMEM((2, 128), F32),
            pltpu.VMEM((group, 2, 128), F32),
            pltpu.VMEM((group, ROWS, depth), F32),
            pltpu.VMEM((2, group, ROWS, depth), F32),
            pltpu.VMEM((group, ROWS, depth), F32),
            pltpu.VMEM((2, group, ROWS, depth), F32),
            pltpu.VMEM((group, ROWS, depth), F32),
            pltpu.VMEM((group, ROWS, depth), F32),
            pltpu.VMEM((n_case - 1, LIVE, 128), F32),
            pltpu.VMEM((LIVE, 128), F32),
            pltpu.SemaphoreType.DMA((4,)),
            pltpu.SemaphoreType.DMA((4,)),
            pltpu.SemaphoreType.DMA((7,)),
            pltpu.SemaphoreType.DMA((7,)),
            pltpu.SemaphoreType.DMA((n_case - 1,)),
            pltpu.SemaphoreType.DMA((n_case - 1,)),
        ],
        compiler_params=pltpu.CompilerParams(
            collective_id=0, has_side_effects=True, vmem_limit_bytes=60 * 1024 * 1024
        ),
        name="flow_step",
    )(
        velocity,
        target,
        weight_in.T,
        bias_in[None, :],
        weight_mid,
        bias_mid[None, :],
        weight_out,
        bias_out,
        thrust_coef[None, :],
        tile_cells,
        tile_turbine,
        tile_weight,
        *tables,
    )
    outs = pl.pallas_call(
        hand_over,
        out_shape=tuple(jax.ShapeDtypeStruct(out.shape, out.dtype) for out in outs),
        in_specs=[vmem] * len(outs),
        out_specs=(vmem,) * len(outs),
        compiler_params=pltpu.CompilerParams(vmem_limit_bytes=60 * 1024 * 1024),
        name="hand_over",
    )(*outs)
    new, loss, step_in, step_bin, step_mid, step_bmid, step_out, step_bout, force = outs
    return (
        new,
        loss[0, 0],
        step_in.T,
        step_bin[0],
        step_mid,
        step_bmid[0],
        step_out,
        step_bout[0],
        force,
    )


def solution(mesh):
    placed = (
        P("case", None, "gx", "gy", None),
        P("case", None, "gx", "gy", None),
        P(),
        P(),
        P(),
        P(),
        P(),
        P(),
        P(),
        P(("gx", "gy"), None),
        P(("gx", "gy")),
        P(("gx", "gy"), None),
    )
    return jax.shard_map(
        on_device,
        mesh=mesh,
        in_specs=placed,
        out_specs=(
            P("case", None, "gx", "gy", None),
            P(),
            P(),
            P(),
            P(),
            P(),
            P(),
            P(),
            P("case", None, "gx", "gy", None),
        ),
        check_vma=False,
    )
```

```python
import functools
import math

import jax
import jax.numpy as jnp
import numpy as np
from jax import lax
from jax.experimental import pallas as pl
from jax.experimental.pallas import tpu as pltpu
from jax.sharding import PartitionSpec as P

ITERS = 20
MESH = pl.DeviceIdType.MESH
F32 = jnp.float32
BF16 = jnp.bfloat16

inflow = 1.0
step_dt = 0.4
viscosity = 0.1
epsilon_rms = 1e-06

ROWS = 24
LIVE = 18
SLOTS = 32
FIRST = 8
STEP = 4
CHANNELS = 16
FEATS = 12


def sines(count):
    index = np.arange(1, count + 1, dtype=np.float64)
    return math.sqrt(2.0 / (count + 1)) * np.sin(math.pi * np.outer(index, index) / (count + 1))


def cosines(count):
    return 2.0 * np.cos(math.pi * np.arange(1, count + 1, dtype=np.float64) / (count + 1))


def solve_tables(n_gx, n_gy, span_x, span_y, depth):
    nx, ny = n_gx * span_x, n_gy * span_y
    group = n_gx * n_gy
    modes = depth // group
    base_x, base_y = sines(nx), sines(ny)
    in_y = np.zeros((n_gy, modes, SLOTS, modes, ny))
    for gy in range(n_gy):
        for slot in range(FIRST - 1, FIRST + span_y + 1):
            y = gy * span_y + slot - FIRST
            if 0 <= y < ny:
                for mode in range(modes):
                    in_y[gy, mode, slot, mode] = base_y[y]
    in_y = in_y.reshape(n_gy * modes * SLOTS, modes * ny)
    in_x = np.zeros((nx, n_gx, ROWS))
    for gx in range(n_gx):
        for row in range(LIVE):
            x = gx * span_x + (row if row < span_x else (-1 if row == span_x else span_x))
            if 0 <= x < nx:
                in_x[:, gx, row] = base_x[x]
    in_x = in_x.reshape(nx, n_gx * ROWS)
    plane = np.tile((cosines(nx)[:, None] + cosines(ny)[None, :]) / 6.0, (1, modes))
    level = np.repeat((cosines(depth) / 6.0).reshape(modes, group).T, ny, axis=1)
    tables = (sines(depth), in_y, in_y.T, in_x, in_x.T, plane, level[:, None, :])
    return tuple(np.ascontiguousarray(table, dtype=np.float32) for table in tables)


def split_two(values):
    high = values.astype(BF16)
    return high, (values - high.astype(F32)).astype(BF16)


def dot_full(left, right):
    left_high, left_low = split_two(left)
    right_high, right_low = split_two(right)
    return (
        jnp.dot(left_low, right_high, preferred_element_type=F32)
        + jnp.dot(left_high, right_low, preferred_element_type=F32)
    ) + jnp.dot(left_high, right_high, preferred_element_type=F32)


def depth_difference(values):
    dim = values.ndim - 1
    depth = values.shape[dim]
    lane = lax.broadcasted_iota(jnp.int32, values.shape, dim)
    above = jnp.where(lane == depth - 1, 0.0, pltpu.roll(values, depth - 1, dim))
    below = jnp.where(lane == 0, 0.0, pltpu.roll(values, 1, dim))
    return above - below


def swap_groups(pieces, stride):
    count = len(pieces)
    lane = lax.broadcasted_iota(jnp.int32, pieces[0].shape, 1) // stride
    results = []
    for b in range(count):
        result = None
        for a in range(count):
            shift = ((a - b) * stride) % (count * stride)
            moved = pieces[a] if shift == 0 else pltpu.roll(pieces[a], shift, 1)
            result = moved if result is None else jnp.where(lane == a, moved, result)
        results.append(result)
    return results


def mm(left, right):
    return jnp.dot(left, right, preferred_element_type=F32)


def mm_cells(left, right):
    return lax.dot_general(left, right, (((1,), (1,)), ((), ())), preferred_element_type=F32)


def split_three(values):
    high = values.astype(BF16)
    rest = values - high.astype(F32)
    middle = rest.astype(BF16)
    low = (rest - middle.astype(F32)).astype(BF16)
    return high, middle, low


def column(row):
    return jnp.broadcast_to(row, (128, row.shape[1])).T[:, 0:1]


def step_kernel(
    sizes,
    v_ref,
    t_ref,
    weight_in,
    bias_in,
    weight_mid,
    bias_mid,
    weight_out,
    bias_out,
    thrust_coef,
    tile_cells,
    tile_turbine,
    tile_weight,
    base_z,
    in_y,
    out_y,
    in_x,
    out_x,
    plane,
    level,
    new_ref,
    loss_ref,
    step_in,
    step_bin,
    step_mid,
    step_bmid,
    step_out,
    step_bout,
    force_ref,
    rext,
    pext,
    vpad,
    tend,
    field,
    gain,
    features,
    one,
    two,
    stage,
    forces,
    result,
    w_one,
    w_out,
    w_mid_back,
    w_out_back,
    b_mid,
    coef,
    g_mid,
    g_out,
    g_in,
    g_bias,
    columns,
    small,
    halo_send,
    halo_x,
    halo_y,
    disk_send,
    disk_recv,
    send_a,
    recv_a,
    send_b,
    recv_b,
    recv_c,
    recv_d,
    cross,
    mine,
    halo_ssem,
    halo_rsem,
    send_sem,
    recv_sem,
    cross_ssem,
    cross_rsem,
):
    n_case, n_gx, n_gy = sizes
    case, gx, gy = lax.axis_index("case"), lax.axis_index("gx"), lax.axis_index("gy")
    group = n_gx * n_gy
    me = gy * n_gx + gx
    span_x, span_y, depth = v_ref.shape[2:]
    modes = depth // group
    units = weight_mid.shape[0]
    last = FIRST + span_y
    steps = span_x // STEP
    lines = STEP * span_y

    def device(index):
        return (case, lax.rem(index, n_gx), index // n_gx)

    for side in range(2):
        recv_a[side, :, span_x:, :] = jnp.zeros((group, ROWS - span_x, depth), F32)

    barrier = pltpu.get_barrier_semaphore()

    def greet(step, carry):
        pl.semaphore_signal(
            barrier,
            inc=1,
            device_id=device(lax.rem(me + step, group)),
            device_id_type=MESH,
        )
        return carry

    lax.fori_loop(1, group, greet, 0)
    for step in range(1, n_case):
        pl.semaphore_signal(
            barrier,
            inc=1,
            device_id=(lax.rem(case + step, n_case), gx, gy),
            device_id_type=MESH,
        )

    row_z = lax.broadcasted_iota(jnp.int32, (depth, 128), 0)
    row_xy = lax.broadcasted_iota(jnp.int32, (span_x * span_y, 128), 0)
    lane = lax.broadcasted_iota(jnp.int32, (1, 128), 1)
    tiles = tile_cells.shape[0]
    stream = v_ref[0, 0].reshape(span_x * span_y, depth)
    disk_sum = jnp.zeros((1, 128), F32)
    disk_area = jnp.zeros((1, 128), F32)
    for tile in range(tiles):
        cells = tile_cells[tile : tile + 1, :]
        weights = tile_weight[tile : tile + 1, :]
        pick_z = jnp.where(row_z == cells % depth, 1.0, 0.0).astype(BF16)
        levels = mm(stream, pick_z)
        sampled = jnp.sum(jnp.where(row_xy == cells // depth, levels, 0.0), 0, keepdims=True)
        weighted = jnp.sum(weights * (sampled + inflow), 1, keepdims=True)
        area = jnp.sum(weights, 1, keepdims=True)
        match = lane == tile_turbine[tile]
        disk_sum = disk_sum + jnp.where(match, weighted, 0.0)
        disk_area = disk_area + jnp.where(match, area, 0.0)
    disk_send[0:1, :] = disk_sum
    disk_send[1:2, :] = disk_area

    vpad[...] = jnp.zeros_like(vpad)
    for component in range(3):
        values = v_ref[0, component].astype(F32)
        vpad[component, 1 : span_x + 1, FIRST:last, :] = values
        halo_send[0, component] = values[:, 0, :].astype(BF16)
        halo_send[1, component] = values[:, span_y - 1, :].astype(BF16)

    stack = [weight_in[...].astype(F32)] + [
        part.astype(F32) for part in split_three(bias_in[...])
    ]
    stack.append(jnp.zeros((CHANNELS - FEATS - 3, units), F32))
    w_one[...] = jnp.concatenate(stack, 0).T.astype(BF16)
    w_out[...] = jnp.zeros_like(w_out)
    w_out[0:3, :] = weight_out[...].astype(F32)
    w_out_back[...] = w_out[...].T.astype(BF16)
    w_mid_back[...] = weight_mid[...].astype(F32).T.astype(BF16)
    b_mid[...] = column(bias_mid[...])
    coef[...] = jnp.zeros_like(coef)
    coef[0:1, 0 : thrust_coef.shape[1]] = thrust_coef[...]
    line_row = lax.broadcasted_iota(jnp.int32, stage.shape, 1)
    stage[...] = jnp.where((line_row >= FEATS) & (line_row < FEATS + 3), 1.0, 0.0)
    forces[...] = jnp.zeros_like(forces)

    ratio = plane[...] + level[me]
    total = jnp.ones_like(ratio)
    for _ in range(ITERS - 1):
        total = total * ratio + 1.0
    gain[...] = total * (-1.0 / 24.0)
    rext[...] = jnp.zeros_like(rext)

    pl.semaphore_wait(barrier, group - 1 + n_case - 1)

    copies = []
    for side, (source, place) in enumerate(((span_x - 1, 1), (0, n_gx - 1))):
        copies.append(
            pltpu.make_async_remote_copy(
                src_ref=v_ref.at[0, :, source],
                dst_ref=halo_x.at[side],
                send_sem=halo_ssem.at[side],
                recv_sem=halo_rsem.at[side],
                device_id=(case, lax.rem(gx + place, n_gx), gy),
                device_id_type=MESH,
            )
        )
    for side, (source, place) in enumerate(((1, 1), (0, n_gy - 1))):
        copies.append(
            pltpu.make_async_remote_copy(
                src_ref=halo_send.at[source],
                dst_ref=halo_y.at[side],
                send_sem=halo_ssem.at[2 + side],
                recv_sem=halo_rsem.at[2 + side],
                device_id=(case, gx, lax.rem(gy + place, n_gy)),
                device_id_type=MESH,
            )
        )
    for copy in copies:
        copy.start()

    def send_disk(step, carry):
        peer = lax.rem(me + step, group)
        pltpu.make_async_remote_copy(
            src_ref=disk_send,
            dst_ref=disk_recv.at[me],
            send_sem=send_sem.at[6],
            recv_sem=recv_sem.at[6],
            device_id=device(peer),
            device_id_type=MESH,
        ).start()
        return carry

    lax.fori_loop(1, group, send_disk, 0)
    disk_recv[me] = disk_send[...]

    for copy in copies:
        copy.wait()
    for component in range(3):
        for side, (row, inside) in enumerate(((0, gx > 0), (span_x + 1, gx < n_gx - 1))):
            values = halo_x[side, component].astype(F32)
            vpad[component, row, FIRST:last, :] = jnp.where(inside, values, 0.0)
        for side, (slot, inside) in enumerate(((FIRST - 1, gy > 0), (last, gy < n_gy - 1))):
            values = halo_y[side, component].astype(F32)
            vpad[component, 1 : span_x + 1, slot, :] = jnp.where(inside, values, 0.0)

    def forward(step, carry):
        base = step * STEP
        rows = pl.ds(base + 1, STEP)
        tendency = []
        speeds = []
        slopes = []
        for component in range(3):
            middle = vpad[component, rows, FIRST:last, :]
            above_x = vpad[component, pl.ds(base + 2, STEP), FIRST:last, :]
            below_x = vpad[component, pl.ds(base, STEP), FIRST:last, :]
            above_y = vpad[component, rows, FIRST + 1 : last + 1, :]
            below_y = vpad[component, rows, FIRST - 1 : last - 1, :]
            level_of = lax.broadcasted_iota(jnp.int32, middle.shape, 2)
            above_z = jnp.where(level_of == depth - 1, 0.0, pltpu.roll(middle, depth - 1, 2))
            below_z = jnp.where(level_of == 0, 0.0, pltpu.roll(middle, 1, 2))
            slopes.append(
                [
                    0.5 * (above_x - below_x),
                    0.5 * (above_y - below_y),
                    0.5 * (above_z - below_z),
                ]
            )
            around = above_x + below_x + above_y + below_y + above_z + below_z
            tendency.append(viscosity * (around - 6.0 * middle))
            speeds.append(middle)
        for component in range(3):
            for axis in range(3):
                stage[:, axis * 3 + component, :] = slopes[component][axis].reshape(lines, depth)
            stage[:, 9 + component, :] = speeds[component].reshape(lines, depth)
            advect = (
                (speeds[0] + inflow) * slopes[component][0]
                + speeds[1] * slopes[component][1]
                + speeds[2] * slopes[component][2]
            )
            tendency[component] = tendency[component] - advect
        for line in range(lines):
            features[step, :, line * depth : (line + 1) * depth] = stage[line].astype(BF16)
        inputs = features[step]
        hidden_one = jnp.tanh(mm(w_one[...], inputs)).astype(BF16)
        one[step] = hidden_one
        hidden_two = jnp.tanh(mm(weight_mid[...], hidden_one) + b_mid[...]).astype(BF16)
        two[step] = hidden_two
        closure = mm(w_out[...].astype(BF16), hidden_two)
        for line in range(lines):
            result[line] = closure[0:8, line * depth : (line + 1) * depth]
        for component in range(3):
            added = result[:, component, :].reshape(STEP, span_y, depth) + bias_out[component]
            tend[component, pl.ds(base, STEP)] = tendency[component] + added
        return carry

    lax.fori_loop(0, steps, forward, 0)

    landed = disk_recv.at[pl.ds(0, group - 1)]
    pltpu.make_async_copy(landed, landed, recv_sem.at[6]).wait()
    pltpu.make_async_copy(landed, landed, send_sem.at[6]).wait()
    disks = jnp.sum(disk_recv[...], 0)
    disk_speed = disks[0:1, :] / jnp.maximum(disks[1:2, :], 1.0)
    thrust = -0.5 * coef[0:1, :] * disk_speed * jnp.abs(disk_speed)
    pushed = jnp.zeros((span_x * span_y, depth), F32)
    for tile in range(tiles):
        cells = tile_cells[tile : tile + 1, :]
        row_thrust = jnp.sum(
            jnp.where(lane == tile_turbine[tile], thrust, 0.0), 1, keepdims=True
        )
        spread = tile_weight[tile : tile + 1, :] * row_thrust
        pick_xy = jnp.where(row_xy == cells // depth, 1.0, 0.0).astype(BF16)
        placed = jnp.where(row_z == cells % depth, spread, 0.0)
        for part in split_three(placed):
            pushed = pushed + mm_cells(pick_xy, part)
    tend[0] = tend[0] + pushed.reshape(span_x, span_y, depth)
    for component in range(3):
        speed = vpad[component, 1 : span_x + 1, FIRST:last, :]
        provisional = (speed + step_dt * tend[component]).astype(BF16)
        tend[component] = provisional.astype(F32)

    def exchange(number, outgoing, incoming, same=False):
        def start(step, carry):
            peer = lax.rem(me + step, group)
            source = outgoing if same else outgoing.at[peer]
            pltpu.make_async_remote_copy(
                src_ref=source.at[pl.ds(0, LIVE)],
                dst_ref=incoming.at[me, pl.ds(0, LIVE)],
                send_sem=send_sem.at[number],
                recv_sem=recv_sem.at[number],
                device_id=device(peer),
                device_id_type=MESH,
            ).start()
            return carry

        lax.fori_loop(1, group, start, 0)
        if same:
            incoming[me, pl.ds(0, LIVE)] = outgoing[pl.ds(0, LIVE)]
        else:
            incoming[me, pl.ds(0, LIVE)] = outgoing[me, pl.ds(0, LIVE)]
        landed = incoming.at[pl.ds(0, group - 1), pl.ds(0, LIVE)]
        pltpu.make_async_copy(landed, landed, recv_sem.at[number]).wait()

    def sent(number):
        left = send_a.at[pl.ds(0, group - 1), pl.ds(0, LIVE)]
        pltpu.make_async_copy(left, left, send_sem.at[number]).wait()

    def solve(number, q_x, q_y, q_z):
        zero_x = jnp.zeros((1, span_y, depth), F32)
        inner = jnp.concatenate([q_x[1:], zero_x], 0) - jnp.concatenate([zero_x, q_x[:-1]], 0)
        inner = inner + depth_difference(q_z)
        wide = jnp.concatenate(
            [
                jnp.zeros((span_x, FIRST, depth), F32),
                q_y,
                jnp.zeros((span_x, SLOTS - last, depth), F32),
            ],
            1,
        )
        rext[0:span_x] = pltpu.roll(wide, SLOTS - 1, 1) - pltpu.roll(wide, 1, 1)
        rext[0:span_x, FIRST:last, :] = rext[0:span_x, FIRST:last, :] + inner
        rext[span_x, FIRST:last, :] = q_x[0]
        rext[span_x + 1, FIRST:last, :] = -q_x[span_x - 1]
        if number > 0:
            sent(2 * number - 2)
        for part in range(rext.shape[0] // modes):
            cells = rext[part * modes : (part + 1) * modes].reshape(modes * SLOTS, depth)
            turned = dot_full(cells, base_z[...]).T
            pieces = [turned[m * group : (m + 1) * group] for m in range(modes)]
            for inside, piece in enumerate(swap_groups(pieces, SLOTS)):
                if part * modes + inside < LIVE:
                    send_a[:, part * modes + inside, :] = piece
        arrived = recv_a.at[number]
        exchange(2 * number, send_a, arrived)
        along_y = None
        for block in range(n_gy):
            rows = arrived[block * n_gx : (block + 1) * n_gx].reshape(n_gx * ROWS, depth)
            part = dot_full(rows, in_y[block * depth : (block + 1) * depth, :])
            along_y = part if along_y is None else along_y + part
        spectrum = dot_full(in_x[...], along_y) * gain[...]
        back = dot_full(out_x[...], spectrum)
        if number > 0:
            sent(2 * number - 1)
        arrived = recv_b.at[number]
        for block in range(n_gy):
            part = dot_full(back, out_y[:, block * depth : (block + 1) * depth])
            send_b[block * n_gx : (block + 1) * n_gx] = part.reshape(n_gx, ROWS, depth)
        exchange(2 * number + 1, send_b, arrived)
        for part in range(pext.shape[0] // modes):
            pieces = [
                arrived[:, min(part * modes + inside, LIVE - 1), :] for inside in range(modes)
            ]
            turned = jnp.concatenate(swap_groups(pieces, SLOTS), 0).T
            pext[part * modes : (part + 1) * modes] = dot_full(turned, base_z[...]).reshape(
                modes, SLOTS, depth
            )

    def slope():
        middle = pext[0:span_x, FIRST:last, :]
        low = pext[span_x : span_x + 1, FIRST:last, :]
        high = pext[span_x + 1 : span_x + 2, FIRST:last, :]
        along_x = jnp.concatenate([middle[1:], high], 0) - jnp.concatenate([low, middle[:-1]], 0)
        along_y = (
            pext[0:span_x, FIRST + 1 : last + 1, :] - pext[0:span_x, FIRST - 1 : last - 1, :]
        )
        return along_x, along_y, depth_difference(middle)

    solve(0, tend[0], tend[1], tend[2])
    cost = jnp.zeros((1, depth), F32)
    for component, change in enumerate(slope()):
        updated = tend[component] - change
        new_ref[0, component] = updated.astype(BF16)
        mismatch = updated - t_ref[0, component].astype(F32)
        cost = cost + jnp.sum(
            (mismatch * mismatch).reshape(span_x * span_y, depth), 0, keepdims=True
        )
        field[component] = 2.0 * mismatch
    small[...] = jnp.zeros_like(small)
    small[43:44, :] = cost
    solve(1, field[0], field[1], field[2])
    for component, change in enumerate(slope()):
        force = (step_dt * (field[component] - change)).astype(BF16)
        force_ref[0, component] = force
        force = force.astype(F32)
        field[component] = force
        small[40 + component : 41 + component, :] = jnp.sum(
            force.reshape(span_x * span_y, depth), 0, keepdims=True
        )

    g_mid[...] = jnp.zeros_like(g_mid)
    g_out[...] = jnp.zeros_like(g_out)
    g_in[...] = jnp.zeros_like(g_in)
    g_bias[...] = jnp.zeros_like(g_bias)

    share = 2 * CHANNELS
    packed = depth // share
    own_lane = lax.broadcasted_iota(jnp.int32, (depth, depth), 1) // share

    def backward(step, carry):
        base = step * STEP
        for component in range(3):
            forces[:, component, :] = field[component, pl.ds(base, STEP)].reshape(lines, depth)
        parts = []
        for first in range(0, lines, packed):
            rows = []
            for line in range(first, first + packed):
                parts.append(forces[line].astype(BF16))
                rows.append(forces[line])
                rows.append(features[step, :, line * depth : (line + 1) * depth].astype(F32))
            turned = jnp.concatenate(rows, 0).T
            for place in range(packed):
                line = first + place
                columns[line * depth : (line + 1) * depth, :] = jnp.where(
                    own_lane == place, turned, 0.0
                ).astype(BF16)
        force = jnp.concatenate(parts, 1)
        hidden_two = two[step]
        hidden_one = one[step]
        value = hidden_two.astype(F32)
        delta_two = (mm(w_out_back[...], force) * (1.0 - value * value)).astype(BF16)
        g_out[...] = g_out[...] + mm(hidden_two, columns[...])
        g_mid[...] = g_mid[...] + mm_cells(hidden_one, delta_two)
        tall = g_bias[...]
        for line in range(lines):
            tall = tall + delta_two[:, line * depth : (line + 1) * depth].astype(F32)
        g_bias[...] = tall
        value = hidden_one.astype(F32)
        delta_one = (mm(w_mid_back[...], delta_two) * (1.0 - value * value)).astype(BF16)
        g_in[...] = g_in[...] + mm(delta_one, columns[...])
        return carry

    lax.fori_loop(0, steps, backward, 0)

    sent(2)
    def folded(sums):
        rows = sums.T
        total = rows[0:share]
        for place in range(1, packed):
            total = total + rows[place * share : (place + 1) * share]
        return total

    for_in = folded(g_in[...])[CHANNELS:share]
    for_out = folded(g_out[...])[0:CHANNELS]
    for_bias = jnp.sum(g_bias[...].T, 0, keepdims=True)
    for half in range(2):
        lanes = slice(half * 128, half * 128 + 128)
        small[half * CHANNELS : (half + 1) * CHANNELS, :] = for_in[:, lanes]
        small[32 + half : 33 + half, :] = for_bias[:, lanes]
        small[34 + 3 * half : 37 + 3 * half, :] = for_out[0:3, lanes]
    middle = g_mid[...].T
    for owner in range(group):
        tile = middle[owner * 8 : (owner + 1) * 8, :]
        send_a[owner, 0:8, :] = tile[:, 0:128]
        send_a[owner, 8:16, :] = tile[:, 128:256]
        send_a[owner, 16:18, :] = small[2 * owner : 2 * owner + 2, :]
    exchange(4, send_a, recv_c)
    mine[...] = jnp.sum(recv_c[:, 0:LIVE, :], 0)
    copies = []
    for step in range(1, n_case):
        copies.append(
            pltpu.make_async_remote_copy(
                src_ref=mine,
                dst_ref=cross.at[step - 1],
                send_sem=cross_ssem.at[step - 1],
                recv_sem=cross_rsem.at[step - 1],
                device_id=(lax.rem(case + step, n_case), gx, gy),
                device_id_type=MESH,
            )
        )
    for copy in copies:
        copy.start()
    for copy in copies:
        copy.wait()
    places = []
    for source in range(n_case):
        step = lax.rem(case - source + n_case, n_case)
        there = cross[lax.max(step - 1, 0)]
        places.append(jnp.where(step == 0, mine[...], there))
    whole = places[0]
    for place in places[1:]:
        whole = whole + place
    sent(3)
    send_b[0, 0:LIVE, :] = whole
    exchange(5, send_b.at[0], recv_d, True)
    for owner in range(group):
        small[2 * owner : 2 * owner + 2, :] = recv_d[owner, 16:18, :]
    big = recv_d[:, 0:16, :].reshape(group * 16, 128)
    rest = small[...]
    bout = jnp.sum(rest[40:43], 1, keepdims=True)
    cost = jnp.sum(rest[43:44], 1, keepdims=True)
    row = lax.broadcasted_iota(jnp.int32, rest.shape, 0)
    inner_row = row % CHANNELS
    counted = ((row < 32) & (inner_row <= FEATS)) | ((row >= 32) & (row < 40))
    kept = jnp.where(counted, rest, 0.0)
    squares = jnp.sum(jnp.sum(big * big, 0, keepdims=True), 1, keepdims=True)
    squares = squares + jnp.sum(jnp.sum(kept * kept, 0, keepdims=True), 1, keepdims=True)
    squares = squares + jnp.sum(bout * bout, 0, keepdims=True)
    entries = units * FEATS + units + units * units + units + 3 * units + 3
    scale_rms = jnp.sqrt(squares / entries + epsilon_rms)
    for owner in range(group):
        step_mid[owner * 8 : (owner + 1) * 8, 0:128] = recv_d[owner, 0:8, :] / scale_rms
        step_mid[owner * 8 : (owner + 1) * 8, 128:256] = recv_d[owner, 8:16, :] / scale_rms
    scaled = rest / scale_rms
    for half in range(2):
        lanes = slice(half * 128, half * 128 + 128)
        block = scaled[half * CHANNELS : (half + 1) * CHANNELS, :]
        step_in[:, lanes] = block[0:FEATS, :]
        step_bin[0:1, lanes] = block[FEATS : FEATS + 1, :]
        step_bmid[0:1, lanes] = scaled[32 + half : 33 + half, :]
        step_out[:, lanes] = scaled[34 + 3 * half : 37 + 3 * half, :]
    diagonal = lax.broadcasted_iota(jnp.int32, (3, 128), 0) == lax.broadcasted_iota(
        jnp.int32, (3, 128), 1
    )
    flat = jnp.sum(jnp.where(diagonal, bout / scale_rms, 0.0), 0, keepdims=True)
    step_bout[...] = flat[:, 0:3]
    cells_all = 3 * n_case * group * span_x * span_y * depth
    loss_ref[...] = cost / cells_all
    sent(4)
    sent(5)


def hand_over(*refs):
    count = len(refs) // 2
    for source, target in zip(refs[:count], refs[count:]):
        target[...] = source[...]


def on_device(
    velocity,
    target,
    weight_in,
    bias_in,
    weight_mid,
    bias_mid,
    weight_out,
    bias_out,
    thrust_coef,
    tile_cells,
    tile_turbine,
    tile_weight,
):
    sizes = tuple(lax.axis_size(axis) for axis in ("case", "gx", "gy"))
    n_case, n_gx, n_gy = sizes
    group = n_gx * n_gy
    _, _, span_x, span_y, depth = velocity.shape
    units = weight_mid.shape[0]
    tables = solve_tables(n_gx, n_gy, span_x, span_y, depth)
    vmem = pl.BlockSpec(memory_space=pltpu.VMEM)
    smem = pl.BlockSpec(memory_space=pltpu.SMEM)
    steps = span_x // STEP
    lines = STEP * span_y
    wide = lines * depth
    outs = pl.pallas_call(
        functools.partial(step_kernel, sizes),
        out_shape=(
            jax.ShapeDtypeStruct(velocity.shape, BF16),
            jax.ShapeDtypeStruct((1, 1), F32),
            jax.ShapeDtypeStruct((FEATS, units), F32),
            jax.ShapeDtypeStruct((1, units), F32),
            jax.ShapeDtypeStruct((units, units), F32),
            jax.ShapeDtypeStruct((1, units), F32),
            jax.ShapeDtypeStruct((3, units), F32),
            jax.ShapeDtypeStruct((1, 3), F32),
            jax.ShapeDtypeStruct(velocity.shape, BF16),
        ),
        in_specs=[vmem] * 7 + [smem, vmem, vmem, smem, vmem] + [vmem] * len(tables),
        out_specs=(vmem,) * 9,
        scratch_shapes=[
            pltpu.VMEM((span_x + 4, SLOTS, depth), F32),
            pltpu.VMEM((span_x + 4, SLOTS, depth), F32),
            pltpu.VMEM((3, span_x + 2, SLOTS, depth), F32),
            pltpu.VMEM((3, span_x, span_y, depth), F32),
            pltpu.VMEM((3, span_x, span_y, depth), F32),
            pltpu.VMEM(tables[5].shape, F32),
            pltpu.VMEM((steps, CHANNELS, wide), BF16),
            pltpu.VMEM((steps, units, wide), BF16),
            pltpu.VMEM((steps, units, wide), BF16),
            pltpu.VMEM((lines, CHANNELS, depth), F32),
            pltpu.VMEM((lines, CHANNELS, depth), F32),
            pltpu.VMEM((lines, 8, depth), F32),
            pltpu.VMEM((units, CHANNELS), BF16),
            pltpu.VMEM((CHANNELS, units), F32),
            pltpu.VMEM((units, units), BF16),
            pltpu.VMEM((units, CHANNELS), BF16),
            pltpu.VMEM((units, 1), F32),
            pltpu.VMEM((8, 128), F32),
            pltpu.VMEM((units, units), F32),
            pltpu.VMEM((units, depth), F32),
            pltpu.VMEM((units, depth), F32),
            pltpu.VMEM((units, depth), F32),
            pltpu.VMEM((wide, depth), BF16),
            pltpu.VMEM((2 * group, 128), F32),
            pltpu.VMEM((2, 3, span_x, depth), BF16),
            pltpu.VMEM((2, 3, span_y, depth), BF16),
            pltpu.VMEM((2, 3, span_x, depth), BF16),
            pltpu.VMEM((2, 128), F32),
            pltpu.VMEM((group, 2, 128), F32),
            pltpu.VMEM((group, ROWS, depth), F32),
            pltpu.VMEM((2, group, ROWS, depth), F32),
            pltpu.VMEM((group, ROWS, depth), F32),
            pltpu.VMEM((2, group, ROWS, depth), F32),
            pltpu.VMEM((group, ROWS, depth), F32),
            pltpu.VMEM((group, ROWS, depth), F32),
            pltpu.VMEM((n_case - 1, LIVE, 128), F32),
            pltpu.VMEM((LIVE, 128), F32),
            pltpu.SemaphoreType.DMA((4,)),
            pltpu.SemaphoreType.DMA((4,)),
            pltpu.SemaphoreType.DMA((7,)),
            pltpu.SemaphoreType.DMA((7,)),
            pltpu.SemaphoreType.DMA((n_case - 1,)),
            pltpu.SemaphoreType.DMA((n_case - 1,)),
        ],
        compiler_params=pltpu.CompilerParams(
            collective_id=0, has_side_effects=True, vmem_limit_bytes=60 * 1024 * 1024
        ),
        name="flow_step",
    )(
        velocity,
        target,
        weight_in.T,
        bias_in[None, :],
        weight_mid,
        bias_mid[None, :],
        weight_out,
        bias_out,
        thrust_coef[None, :],
        tile_cells,
        tile_turbine,
        tile_weight,
        *tables,
    )
    outs = pl.pallas_call(
        hand_over,
        out_shape=tuple(jax.ShapeDtypeStruct(out.shape, out.dtype) for out in outs),
        in_specs=[vmem] * len(outs),
        out_specs=(vmem,) * len(outs),
        compiler_params=pltpu.CompilerParams(vmem_limit_bytes=60 * 1024 * 1024),
        name="hand_over",
    )(*outs)
    new, loss, step_in, step_bin, step_mid, step_bmid, step_out, step_bout, force = outs
    return (
        new,
        loss[0, 0],
        step_in.T,
        step_bin[0],
        step_mid,
        step_bmid[0],
        step_out,
        step_bout[0],
        force,
    )


def solution(mesh):
    placed = (
        P("case", None, "gx", "gy", None),
        P("case", None, "gx", "gy", None),
        P(),
        P(),
        P(),
        P(),
        P(),
        P(),
        P(),
        P(("gx", "gy"), None),
        P(("gx", "gy")),
        P(("gx", "gy"), None),
    )
    return jax.shard_map(
        on_device,
        mesh=mesh,
        in_specs=placed,
        out_specs=(
            P("case", None, "gx", "gy", None),
            P(),
            P(),
            P(),
            P(),
            P(),
            P(),
            P(),
            P("case", None, "gx", "gy", None),
        ),
        check_vma=False,
    )
```
